32 devices in a mesh: group: 8 (over z, core), inner: 4 (over y, x).
Axes of the slice: x: 2, y: 2, z: 4, core: 2. Of those that a mesh axis runs over, the one named last changes fastest.
Arguments:
- leaf_blocks: float32 [8192, 256], P(('group', 'inner')), may hold values from -3 to 3, as said below
- bases: float32 [8192, 320], P(('group', 'inner')), may hold values from -2 to 2
- targets: float32 [8192, 128], P(('group', 'inner')), may hold values from -30 to 30
- coupling: float32 [5, 64], replicated, may hold values from 0.01 to 1
Outputs:
- solution: float32 [8192, 128], P(('group', 'inner'))
The draws below stay inside these ranges and needn't reach their ends.
Inputs may be any that keep to these rules, and one draw needn't show every extreme that they name: Each leaf block of leaf_blocks is symmetric with all eigenvalues at least 0.4.
All inputs are finite; a program needn't handle non-finite values.
Results may differ from the reference program's by a relative error of at most 0.00014.
Values sent between devices are 32-bit elements; how exact they have to be, the bound alone decides.
A program may use at most 64 MiB of HBM per device.

```python
import math
import jax
import jax.numpy as jnp
from jax import lax

M = 256
R = 64
NRHS = 128
LEVELS = 5
BLOCKS = 32
NPTS = 8192


def shared_draw(key):
    scale_key = jax.random.fold_in(key, 101)
    basis_key = jax.random.fold_in(key, 202)
    noise_key = jax.random.fold_in(key, 303)
    latent_key = jax.random.fold_in(key, 404)
    scales = jnp.exp(jax.random.uniform(scale_key, (BLOCKS, 1, LEVELS, 1), jnp.float32, math.log(0.5), math.log(2.0)))
    entries = jnp.clip(jax.random.normal(basis_key, (BLOCKS, M, LEVELS, R), jnp.float32), -5.0, 5.0)
    level_bases = jnp.clip(entries * scales / math.sqrt(M), -2.0, 2.0)
    bases_out = level_bases.reshape(NPTS, LEVELS * R)
    targets_out = jnp.clip(jax.random.normal(noise_key, (NPTS, NRHS), jnp.float32), -6.0, 6.0)
    for current in range(LEVELS):
        node_count = BLOCKS // 2 ** (current + 1)
        level_basis = level_bases[:, :, current, :].reshape(node_count, -1, R)
        latent = 2.0 * jnp.clip(jax.random.normal(jax.random.fold_in(latent_key, current), (node_count, R, NRHS), jnp.float32), -5.0, 5.0)
        targets_out = targets_out + jnp.einsum('nsr,nrc->nsc', level_basis, latent).reshape(NPTS, NRHS)
    return (bases_out, jnp.clip(targets_out, -30.0, 30.0))


def draw_bases(key, part):
    return shared_draw(key)[0]


def draw_targets(key, part):
    return shared_draw(key)[1]


def draw_leaf_blocks(key, part):
    sym_key = jax.random.fold_in(key, 505)
    diag_key = jax.random.fold_in(key, 606)
    raw_part = jnp.clip(jax.random.normal(sym_key, (BLOCKS, M, M), jnp.float32), -5.0, 5.0)
    diagonal = jax.random.uniform(diag_key, (BLOCKS, M), jnp.float32, 1.5, 2.5)
    symmetric = (raw_part + jnp.swapaxes(raw_part, 1, 2)) * (0.35 / math.sqrt(M))
    identity = jnp.eye(M, dtype=jnp.float32)
    return (symmetric + diagonal[:, :, None] * identity).reshape(NPTS, M)


def setup_inputs(seed: int = 0) -> dict:
    splits = jax.random.split(jax.random.key(seed), 5)
    return {
        "leaf_blocks": draw_leaf_blocks(jax.random.fold_in(splits[4], 71), 0),
        "bases": draw_bases(jax.random.fold_in(splits[4], 71), 0),
        "targets": draw_targets(jax.random.fold_in(splits[4], 71), 0),
        "coupling": jnp.clip(jnp.exp(jax.random.uniform(splits[3], (LEVELS, R), jnp.float32, math.log(0.01), math.log(1.0))), 0.01, 1.0),
    }


def chol_solve(factor, rhs_cols):
    forward = lax.linalg.triangular_solve(factor, rhs_cols, left_side=True, lower=True)
    return lax.linalg.triangular_solve(factor, forward, left_side=True, lower=True, transpose_a=True)

def coefficients(gram_part, weights, projected):
    capacity = gram_part + jnp.diag(1.0 / weights)
    capacity = 0.5 * (capacity + capacity.T)
    return chol_solve(jnp.linalg.cholesky(capacity), projected)

def leaf_solve(item_pair):
    block_rows, rhs_cols = item_pair
    return chol_solve(jnp.linalg.cholesky(block_rows), rhs_cols)

def reference(leaf_blocks, bases, targets, coupling):
    blocks = leaf_blocks.reshape(BLOCKS, M, M)
    columns = jnp.concatenate([bases, targets], axis=1).reshape(BLOCKS, M, LEVELS * R + NRHS)
    solved = lax.map(leaf_solve, (blocks, columns)).reshape(NPTS, LEVELS * R + NRHS)
    for current in range(LEVELS):
        node_count = BLOCKS // 2 ** (current + 1)
        width_now = solved.shape[1]
        level_basis = bases[:, current * R:(current + 1) * R].reshape(node_count, -1, R)
        grouped = solved.reshape(node_count, -1, width_now)
        node_sum = jnp.einsum('nsr,nsc->nrc', level_basis, grouped, precision=lax.Precision.HIGHEST)
        solve_coef = jax.vmap(coefficients, in_axes=(0, None, 0))(node_sum[:, :, :R], coupling[current], node_sum[:, :, R:])
        remaining = grouped[:, :, R:] - jnp.einsum('nsr,nrc->nsc', grouped[:, :, :R], solve_coef, precision=lax.Precision.HIGHEST)
        solved = remaining.reshape(NPTS, width_now - R)
    return solved
```

```python
import functools

import jax
import jax.numpy as jnp
from jax import lax
from jax.experimental import pallas as pl
from jax.experimental.pallas import tpu as pltpu
from jax.sharding import PartitionSpec as P

EIGEN_MIN = 0.4
LEAF_TOL = 3e-4
VMEM = pl.BlockSpec(memory_space=pltpu.VMEM)


def mm(first, second):
    return jnp.dot(
        first,
        second,
        precision=lax.Precision.HIGHEST,
        preferred_element_type=jnp.float32,
    )


def mm_t(first, second):
    return lax.dot_general(
        first,
        second,
        (((0,), (0,)), ((), ())),
        precision=lax.Precision.HIGHEST,
        preferred_element_type=jnp.float32,
    )


def identity(size):
    rows = lax.broadcasted_iota(jnp.int32, (size, size), 0)
    cols = lax.broadcasted_iota(jnp.int32, (size, size), 1)
    return jnp.where(rows == cols, 1.0, 0.0).astype(jnp.float32)


def spd_inverse(matrix, low, high, pair_ref):
    size = matrix.shape[0]
    eye = identity(size)
    alpha = 2.0 / (low + high)
    pair_ref[:size, :] = eye - alpha * matrix
    pair_ref[size:, :] = alpha * eye

    def cond(rho):
        return rho > LEAF_TOL

    def body(rho):
        square = rho * rho
        scale = 2.0 / (2.0 - square)
        pair = pair_ref[...]
        product = mm(pair, pair[:size])
        pair_ref[:size, :] = (1.0 - scale) * eye + scale * product[:size]
        pair_ref[size:, :] = scale * (pair[size:] + product[size:])
        return square / (2.0 - square)

    lax.while_loop(cond, body, (high - low) / (high + low))
    inverse = pair_ref[size:, :]
    return inverse + mm(inverse, eye - mm(matrix, inverse))


def leaf_kernel(rank, levels, leaf_ref, bases_ref, targets_ref, solved_ref, *rest):
    blocks, pair_ref = rest[:levels], rest[levels]
    matrix = leaf_ref[...]
    high = jnp.max(jnp.sum(jnp.abs(matrix), axis=0, keepdims=True))
    inverse = spd_inverse(matrix, EIGEN_MIN, jnp.maximum(high, 2 * EIGEN_MIN), pair_ref)
    columns = [targets_ref[...]] + [
        bases_ref[:, rank * level : rank * (level + 1)]
        for level in reversed(range(levels))
    ]
    rhs = jnp.concatenate(columns, axis=1)
    solved = mm(inverse, rhs)
    solved_ref[...] = solved
    gram = mm_t(bases_ref[...], solved)
    for level in range(levels):
        width = solved.shape[1] - rank * level
        blocks[level][...] = gram[rank * level : rank * (level + 1), :width]


def level_kernel(rank, count, current, coupling_ref, *refs):
    own, other = refs[:count], refs[count : 2 * count]
    coef_ref, rest = refs[2 * count], refs[2 * count + 1 : 3 * count]
    pair_ref = refs[3 * count]
    front = own[0][...] + other[0][...]
    width = front.shape[1] - rank
    eye = identity(rank)
    gram = front[:, width:]
    extra = 1.0 / coupling_ref[current : current + 1, :]
    capacity = 0.5 * (gram + gram.T) + eye * extra
    diag_row = jnp.sum(capacity * eye, axis=0, keepdims=True)
    diag_col = jnp.sum(capacity * eye, axis=1, keepdims=True)
    root_row, root_col = lax.rsqrt(diag_row), lax.rsqrt(diag_col)
    scaled = capacity * root_row * root_col
    low = 0.99 * jnp.min(extra / diag_row)
    high = jnp.max(jnp.sum(jnp.abs(scaled), axis=0, keepdims=True))
    inverse = spd_inverse(scaled, low, high, pair_ref)
    projected = front[:, :width]
    coef = root_col * mm(inverse, root_col * projected)
    coef_ref[...] = coef
    if count > 1:
        base = width - rank * (count - 1)
        update = mm_t(projected[:, base:], coef)
        for index in range(1, count):
            rows = rank * (count - 1 - index)
            wide = own[index].shape[1]
            rest[index - 1][...] = (
                own[index][...] + other[index][...]
            ) - update[rows : rows + rank, :wide]


def from_partner(value, axis, distance):
    mask = 2**distance
    pairs = [(source, source ^ mask) for source in range(lax.axis_size(axis))]
    return lax.ppermute(value, axis, pairs)


def per_device(leaf_blocks, bases, targets, coupling):
    levels, rank = coupling.shape
    rows, size = leaf_blocks.shape
    width = targets.shape[1] + rank * levels
    inner_bits = lax.axis_size("inner").bit_length() - 1
    f32 = jnp.float32
    widths = [width - rank * level for level in range(levels)]
    solved, *blocks = pl.pallas_call(
        functools.partial(leaf_kernel, rank, levels),
        out_shape=[jax.ShapeDtypeStruct((rows, width), f32)]
        + [jax.ShapeDtypeStruct((rank, wide), f32) for wide in widths],
        in_specs=[VMEM] * 3,
        out_specs=[VMEM] * (1 + levels),
        scratch_shapes=[pltpu.VMEM((2 * size, size), f32)],
        compiler_params=pltpu.CompilerParams(vmem_limit_bytes=32 * 2**20),
        name="leaf",
    )(leaf_blocks, bases, targets)
    for current in range(levels):
        if current < inner_bits:
            axis, bit = "inner", current
        else:
            axis, bit = "group", current - inner_bits
        others = [from_partner(block, axis, bit) for block in blocks]
        count = levels - current
        wide = widths[current] - rank
        coef, *blocks = pl.pallas_call(
            functools.partial(level_kernel, rank, count, current),
            out_shape=[jax.ShapeDtypeStruct((rank, wide), f32)]
            + [jax.ShapeDtypeStruct(block.shape, f32) for block in blocks[1:]],
            in_specs=[VMEM] * (1 + 2 * count),
            out_specs=[VMEM] * count,
            scratch_shapes=[pltpu.VMEM((2 * rank, rank), f32)],
            compiler_params=pltpu.CompilerParams(vmem_limit_bytes=32 * 2**20),
            name="level",
        )(coupling, *blocks, *others)
        solved = solved[:, :wide] - mm(solved[:, wide:], coef)
    return solved


def solution(mesh):
    rows = P(("group", "inner"), None)
    return jax.shard_map(
        per_device,
        mesh=mesh,
        in_specs=(rows, rows, rows, P()),
        out_specs=rows,
        check_vma=False,
    )
```

```python
import functools
import math

import jax
import jax.numpy as jnp
from jax import lax
from jax.experimental import pallas as pl
from jax.experimental.pallas import tpu as pltpu
from jax.sharding import PartitionSpec as P

EIGEN_MIN = 0.4
LEAF_TOL = 3e-4
VMEM = pl.BlockSpec(memory_space=pltpu.VMEM)


def mm(first, second):
    return jnp.dot(
        first,
        second,
        precision=lax.Precision.HIGHEST,
        preferred_element_type=jnp.float32,
    )


def mm_t(first, second):
    return lax.dot_general(
        first,
        second,
        (((0,), (0,)), ((), ())),
        precision=lax.Precision.HIGHEST,
        preferred_element_type=jnp.float32,
    )


def mm_nt(first, second):
    return lax.dot_general(
        first,
        second,
        (((1,), (1,)), ((), ())),
        precision=lax.Precision.HIGHEST,
        preferred_element_type=jnp.float32,
    )


def identity(size):
    rows = lax.broadcasted_iota(jnp.int32, (size, size), 0)
    cols = lax.broadcasted_iota(jnp.int32, (size, size), 1)
    return jnp.where(rows == cols, 1.0, 0.0).astype(jnp.float32)


def spd_inverse(matrix, low, high, pair_ref):
    size = matrix.shape[0]
    eye = identity(size)
    alpha = 2.0 / (low + high)
    pair_ref[:size, :] = eye - alpha * matrix
    pair_ref[size:, :] = alpha * eye

    def cond(rho):
        return rho > LEAF_TOL

    def body(rho):
        square = rho * rho
        scale = 2.0 / (2.0 - square)
        pair = pair_ref[...]
        product = mm(pair, pair[:size])
        pair_ref[:size, :] = (1.0 - scale) * eye + scale * product[:size]
        pair_ref[size:, :] = scale * (pair[size:] + product[size:])
        return square / (2.0 - square)

    lax.while_loop(cond, body, (high - low) / (high + low))
    inverse = pair_ref[size:, :]
    return inverse + mm(inverse, eye - mm(matrix, inverse))


def leaf_kernel(rank, levels, leaf_ref, bases_ref, targets_ref, solved_ref, *rest):
    blocks, pair_ref = rest[:levels], rest[levels]
    matrix = leaf_ref[...]
    high = jnp.max(jnp.sum(jnp.abs(matrix), axis=0, keepdims=True))
    inverse = spd_inverse(matrix, EIGEN_MIN, jnp.maximum(high, 2 * EIGEN_MIN), pair_ref)
    flipped = jnp.concatenate(
        [
            bases_ref[rank * level : rank * (level + 1), :]
            for level in reversed(range(levels))
        ],
        axis=0,
    )
    solved = jnp.concatenate(
        [mm(inverse, targets_ref[...]), mm_nt(inverse, flipped)], axis=1
    )
    solved_ref[...] = solved
    gram = mm(bases_ref[...], solved)
    for level in range(levels):
        width = solved.shape[1] - rank * level
        blocks[level][...] = gram[rank * level : rank * (level + 1), :width]


def fixed_inverse(matrix, low, high, doublings):
    size = matrix.shape[0]
    eye = identity(size)
    alpha = 2.0 / (low + high)
    rho = (high - low) / (high + low)
    residual = eye - alpha * matrix
    inverse = alpha * eye
    for _ in range(doublings):
        square = rho * rho
        scale = 2.0 / (2.0 - square)
        rho = square / (2.0 - square)
        product = mm(jnp.concatenate([residual, inverse], axis=0), residual)
        inverse = scale * (inverse + product[size:])
        residual = (1.0 - scale) * eye + scale * product[:size]
    return inverse + mm(inverse, eye - mm(matrix, inverse))


def capacity_solve(front, weights, rank, doublings):
    width = front.shape[1] - rank
    eye = identity(rank)
    gram = front[:, width:]
    extra = 1.0 / weights
    capacity = 0.5 * (gram + gram.T) + eye * extra
    diag_row = jnp.sum(capacity * eye, axis=0, keepdims=True)
    diag_col = jnp.sum(capacity * eye, axis=1, keepdims=True)
    root_row, root_col = lax.rsqrt(diag_row), lax.rsqrt(diag_col)
    scaled = capacity * root_row * root_col
    low = 0.99 * jnp.min(extra / diag_row, axis=1, keepdims=True)
    sums = jnp.sum(jnp.abs(scaled), axis=0, keepdims=True)
    high = jnp.max(sums, axis=1, keepdims=True)
    low = jnp.broadcast_to(low, (1, rank))
    high = jnp.broadcast_to(high, (1, rank))
    inverse = fixed_inverse(scaled, low, high, doublings)
    return root_col * mm(inverse, root_col * front[:, :width])


def tree_kernel(rank, levels, inner_bits, doublings, coupling_ref, solved_ref, *refs):
    pairs = [(k, j) for k in range(levels) for j in range(k, levels)]
    number = {pair: index for index, pair in enumerate(pairs)}
    first, refs = refs[:levels], refs[levels:]
    out_ref, state_ref, refs = refs[0], refs[1], refs[2:]
    landed = dict(zip(pairs, refs[: len(pairs)]))
    later = pairs[levels:]
    own = dict(zip(pairs[:levels], first))
    own.update(zip(later, refs[len(pairs) : len(pairs) + len(later)]))
    send_sem, recv_sem = refs[-2:]

    group, inner = lax.axis_index("group"), lax.axis_index("inner")

    def partner(level):
        if level < inner_bits:
            mask = 2**level
            return (group, inner + mask * (1 - 2 * ((inner // mask) % 2)))
        mask = 2 ** (level - inner_bits)
        return (group + mask * (1 - 2 * ((group // mask) % 2)), inner)

    partners = [partner(level) for level in range(levels)]

    def copy_of(k, j):
        return pltpu.make_async_remote_copy(
            src_ref=own[k, j],
            dst_ref=landed[k, j],
            send_sem=send_sem.at[number[k, j]],
            recv_sem=recv_sem.at[number[k, j]],
            device_id=partners[k],
            device_id_type=pl.DeviceIdType.MESH,
        )

    barrier = pltpu.get_barrier_semaphore()
    for other in partners:
        pl.semaphore_signal(
            barrier, inc=1, device_id=other, device_id_type=pl.DeviceIdType.MESH
        )
    pl.semaphore_wait(barrier, levels)

    for j in range(levels):
        copy_of(0, j).start()
    state_ref[...] = solved_ref[...]
    for k in range(levels):
        copy_of(k, k).wait_recv()
        front = own[k, k][...] + landed[k, k][...]
        wide = front.shape[1] - rank
        coef = capacity_solve(front, coupling_ref[k : k + 1, :], rank, doublings)
        if k + 1 < levels:
            base = wide - rank * (levels - 1 - k)
            update = mm_t(front[:, base:wide], coef)
            for j in range(k + 1, levels):
                rows = rank * (levels - 1 - j)
                columns = own[k, j].shape[1]
                copy_of(k, j).wait_recv()
                own[k + 1, j][...] = (own[k, j][...] + landed[k, j][...]) - update[
                    rows : rows + rank, :columns
                ]
                copy_of(k + 1, j).start()
            state_ref[:, :wide] = state_ref[:, :wide] - mm(
                state_ref[:, wide : wide + rank], coef
            )
        else:
            out_ref[...] = state_ref[:, :wide] - mm(
                state_ref[:, wide : wide + rank], coef
            )
    for pair in pairs:
        copy_of(*pair).wait_send()


def per_device(leaf_blocks, bases, targets, coupling):
    levels, rank = coupling.shape
    rows, size = leaf_blocks.shape
    right = targets.shape[1]
    width = right + rank * levels
    inner_bits = lax.axis_size("inner").bit_length() - 1
    f32 = jnp.float32
    widths = [width - rank * level for level in range(levels)]
    solved, *blocks = pl.pallas_call(
        functools.partial(leaf_kernel, rank, levels),
        out_shape=[jax.ShapeDtypeStruct((rows, width), f32)]
        + [jax.ShapeDtypeStruct((rank, wide), f32) for wide in widths],
        in_specs=[VMEM] * 3,
        out_specs=[VMEM] * (1 + levels),
        scratch_shapes=[pltpu.VMEM((2 * size, size), f32)],
        compiler_params=pltpu.CompilerParams(vmem_limit_bytes=32 * 2**20),
        name="leaf",
    )(leaf_blocks, bases.T, targets)
    pairs = [(k, j) for k in range(levels) for j in range(k, levels)]
    landed = [pltpu.VMEM((rank, widths[j]), f32) for _, j in pairs]
    worst = rank * (4.0 * rows * 2**levels / EIGEN_MIN + 1.0)
    doublings = math.ceil(math.log2(math.sqrt(worst) * 4.1))
    return pl.pallas_call(
        functools.partial(tree_kernel, rank, levels, inner_bits, doublings),
        out_shape=jax.ShapeDtypeStruct((rows, right), f32),
        in_specs=[VMEM] * (2 + levels),
        out_specs=VMEM,
        scratch_shapes=[pltpu.VMEM((rows, width), f32)]
        + landed
        + landed[levels:]
        + [pltpu.SemaphoreType.DMA((len(pairs),))] * 2,
        compiler_params=pltpu.CompilerParams(
            collective_id=0, has_side_effects=True, vmem_limit_bytes=40 * 2**20
        ),
        name="tree",
    )(coupling, solved, *blocks)


def solution(mesh):
    rows = P(("group", "inner"), None)
    return jax.shard_map(
        per_device,
        mesh=mesh,
        in_specs=(rows, rows, rows, P()),
        out_specs=rows,
        check_vma=False,
    )
```

```python
import functools
import math

import jax
import jax.numpy as jnp
from jax import lax
from jax.experimental import pallas as pl
from jax.experimental.pallas import tpu as pltpu
from jax.sharding import PartitionSpec as P

EIGEN_MIN = 0.4
LEAF_TOL = 3e-4
RESIDUAL_MAX = 1e-3
FLAG_ROWS = 8
VMEM = pl.BlockSpec(memory_space=pltpu.VMEM)


def mm(first, second):
    return jnp.dot(
        first,
        second,
        precision=lax.Precision.HIGHEST,
        preferred_element_type=jnp.float32,
    )


def split(value):
    high = value.astype(jnp.bfloat16)
    return high, (value - high.astype(jnp.float32)).astype(jnp.bfloat16)


def mm3(first, second):
    (a_high, a_low), (b_high, b_low) = split(first), split(second)
    dot = functools.partial(jnp.dot, preferred_element_type=jnp.float32)
    return dot(a_high, b_high) + (dot(a_high, b_low) + dot(a_low, b_high))


def mm_t(first, second):
    return lax.dot_general(
        first,
        second,
        (((0,), (0,)), ((), ())),
        precision=lax.Precision.HIGHEST,
        preferred_element_type=jnp.float32,
    )


def mm_nt(first, second):
    return lax.dot_general(
        first,
        second,
        (((1,), (1,)), ((), ())),
        precision=lax.Precision.HIGHEST,
        preferred_element_type=jnp.float32,
    )


def identity(size):
    rows = lax.broadcasted_iota(jnp.int32, (size, size), 0)
    cols = lax.broadcasted_iota(jnp.int32, (size, size), 1)
    return jnp.where(rows == cols, 1.0, 0.0).astype(jnp.float32)


def spd_inverse(matrix, low, high, pair_ref):
    size = matrix.shape[0]
    eye = identity(size)
    alpha = 2.0 / (low + high)
    pair_ref[:size, :] = eye - alpha * matrix
    pair_ref[size:, :] = alpha * eye

    def cond(rho):
        return rho > LEAF_TOL

    def body(rho):
        square = rho * rho
        scale = 2.0 / (2.0 - square)
        pair = pair_ref[...]
        product = mm3(pair, pair[:size])
        pair_ref[:size, :] = (1.0 - scale) * eye + scale * product[:size]
        pair_ref[size:, :] = scale * (pair[size:] + product[size:])
        return square / (2.0 - square)

    lax.while_loop(cond, body, (high - low) / (high + low))
    pair_ref[size:, :] = pair_ref[size:, :] + mm(
        pair_ref[size:, :], eye - mm(matrix, pair_ref[size:, :])
    )

    @pl.when(high > 100.0 * low)
    def _():
        for _ in range(2):
            inverse = pair_ref[size:, :]
            pair_ref[size:, :] = inverse + mm(inverse, eye - mm(matrix, inverse))

    return pair_ref[size:, :]


def leaf_kernel(rank, levels, leaf_ref, bases_ref, targets_ref, solved_ref, *rest):
    blocks, pair_ref = rest[:levels], rest[levels]
    matrix = leaf_ref[...]
    high = jnp.max(jnp.sum(jnp.abs(matrix), axis=0, keepdims=True))
    inverse = spd_inverse(matrix, EIGEN_MIN, jnp.maximum(high, 2 * EIGEN_MIN), pair_ref)
    flipped = jnp.concatenate(
        [
            bases_ref[rank * level : rank * (level + 1), :]
            for level in reversed(range(levels))
        ],
        axis=0,
    )
    solved = jnp.concatenate(
        [mm(inverse, targets_ref[...]), mm_nt(inverse, flipped)], axis=1
    )
    solved_ref[...] = solved
    gram = mm(bases_ref[...], solved)
    for level in range(levels):
        width = solved.shape[1] - rank * level
        blocks[level][...] = gram[rank * level : rank * (level + 1), :width]


def fixed_inverse(matrix, low, high, doublings):
    size = matrix.shape[0]
    eye = identity(size)
    alpha = 2.0 / (low + high)
    rho = (high - low) / (high + low)
    residual = eye - alpha * matrix
    inverse = alpha * eye
    for _ in range(doublings):
        square = rho * rho
        scale = 2.0 / (2.0 - square)
        rho = square / (2.0 - square)
        product = mm(jnp.concatenate([residual, inverse], axis=0), residual)
        inverse = scale * (inverse + product[size:])
        residual = (1.0 - scale) * eye + scale * product[:size]
    return inverse + mm(inverse, eye - mm(matrix, inverse))


def quick_solve(matrix, rhs, high):
    size = matrix.shape[0]
    eye = identity(size)
    alpha = 2.0 / (1.0 + high)
    residual = eye - alpha * matrix
    inverse = alpha * (eye + residual)
    residual = mm3(residual, residual)
    for _ in range(2):
        product = mm3(jnp.concatenate([residual, inverse], axis=0), residual)
        inverse = inverse + product[size:]
        residual = product[:size]
    inverse = inverse + mm3(inverse, residual)
    error = eye - mm(inverse, matrix)
    found = mm(inverse, rhs)
    worst = jnp.max(
        jnp.sum(jnp.abs(error), axis=0, keepdims=True), axis=1, keepdims=True
    )
    return found + mm(error, found), worst


def capacity_solve(front, weights, rank, doublings):
    width = front.shape[1] - rank
    eye = identity(rank)
    gram = front[:, width:]
    extra = 1.0 / weights
    capacity = 0.5 * (gram + gram.T) + eye * extra
    diag_row = jnp.sum(capacity * eye, axis=0, keepdims=True)
    diag_col = jnp.sum(capacity * eye, axis=1, keepdims=True)
    root_row, root_col = lax.rsqrt(diag_row), lax.rsqrt(diag_col)
    scaled = capacity * root_row * root_col
    sums = jnp.sum(jnp.abs(scaled), axis=0, keepdims=True)
    high = jnp.broadcast_to(jnp.max(sums, axis=1, keepdims=True), (1, rank))
    rhs = root_col * front[:, :width]
    if not doublings:
        found, worst = quick_solve(scaled, rhs, high)
        return root_col * found, worst
    low = 0.99 * jnp.min(extra / diag_row, axis=1, keepdims=True)
    low = jnp.broadcast_to(low, (1, rank))
    return root_col * mm(fixed_inverse(scaled, low, high, doublings), rhs), None


def tree_kernel(rank, levels, inner_bits, doublings, coupling_ref, solved_ref, *refs):
    pairs = [(k, j) for k in range(levels) for j in range(k, levels)]
    number = {pair: index for index, pair in enumerate(pairs)}
    first, refs = refs[:levels], refs[levels:]
    if doublings:
        (out_ref, state_ref), refs = refs[:2], refs[2:]
    else:
        (out_ref, flag_ref, state_ref), refs = refs[:3], refs[3:]
    landed = dict(zip(pairs, refs[: len(pairs)]))
    later = pairs[levels:]
    own = dict(zip(pairs[:levels], first))
    own.update(zip(later, refs[len(pairs) : len(pairs) + len(later)]))
    send_sem, recv_sem, load_sem = refs[-3:]
    load = pltpu.make_async_copy(solved_ref, state_ref, load_sem)
    load.start()

    group, inner = lax.axis_index("group"), lax.axis_index("inner")

    def partner(level):
        if level < inner_bits:
            mask = 2**level
            return (group, inner + mask * (1 - 2 * ((inner // mask) % 2)))
        mask = 2 ** (level - inner_bits)
        return (group + mask * (1 - 2 * ((group // mask) % 2)), inner)

    partners = [partner(level) for level in range(levels)]

    def copy_of(k, j):
        return pltpu.make_async_remote_copy(
            src_ref=own[k, j],
            dst_ref=landed[k, j],
            send_sem=send_sem.at[number[k, j]],
            recv_sem=recv_sem.at[number[k, j]],
            device_id=partners[k],
            device_id_type=pl.DeviceIdType.MESH,
        )

    barrier = pltpu.get_barrier_semaphore()
    for other in partners:
        pl.semaphore_signal(
            barrier, inc=1, device_id=other, device_id_type=pl.DeviceIdType.MESH
        )
    pl.semaphore_wait(barrier, levels)

    for j in range(levels):
        copy_of(0, j).start()
    bad = jnp.zeros((1, 1), jnp.float32)
    for k in range(levels):
        copy_of(k, k).wait_recv()
        front = own[k, k][:rank, :] + landed[k, k][:rank, :]
        wide = front.shape[1] - rank
        coef, worst = capacity_solve(
            front, coupling_ref[k : k + 1, :], rank, doublings
        )
        if not doublings:
            if k > 0:
                flags = jnp.maximum(own[k, k][rank:, :128], landed[k, k][rank:, :128])
                bad = jnp.max(flags[:1, :], axis=1, keepdims=True)
            bad = jnp.maximum(bad, worst)
        if k + 1 < levels:
            base = wide - rank * (levels - 1 - k)
            update = mm_t(front[:, base:wide], coef)
            for j in range(k + 1, levels):
                rows = rank * (levels - 1 - j)
                columns = own[k, j].shape[1]
                copy_of(k, j).wait_recv()
                own[k + 1, j][:rank, :] = (own[k, j][...] + landed[k, j][...]) - update[
                    rows : rows + rank, :columns
                ]
                if j == k + 1 and not doublings:
                    own[k + 1, j][rank:, :] = jnp.broadcast_to(
                        bad, (FLAG_ROWS, columns)
                    )
                copy_of(k + 1, j).start()
            if k == 0:
                load.wait()
            state_ref[:, :wide] = state_ref[:, :wide] - mm(
                state_ref[:, wide : wide + rank], coef
            )
        else:
            out_ref[...] = state_ref[:, :wide] - mm(
                state_ref[:, wide : wide + rank], coef
            )
    if not doublings:
        flag_ref[...] = jnp.broadcast_to(bad, flag_ref.shape)
    for pair in pairs:
        copy_of(*pair).wait_send()


def call_tree(coupling, solved, blocks, inner_bits, doublings):
    levels, rank = coupling.shape
    rows, width = solved.shape
    right = width - rank * levels
    f32 = jnp.float32
    pairs = [(k, j) for k in range(levels) for j in range(k, levels)]
    extra = 0 if doublings else FLAG_ROWS
    landed = [
        pltpu.VMEM((rank + (extra if j == k > 0 else 0), width - rank * j), f32)
        for k, j in pairs
    ]
    result = [jax.ShapeDtypeStruct((rows, right), f32)]
    if not doublings:
        result.append(jax.ShapeDtypeStruct((FLAG_ROWS, 128), f32))
    return pl.pallas_call(
        functools.partial(tree_kernel, rank, levels, inner_bits, doublings),
        out_shape=result,
        in_specs=[VMEM, pl.BlockSpec(memory_space=pl.ANY)] + [VMEM] * levels,
        out_specs=[VMEM] * len(result),
        scratch_shapes=[pltpu.VMEM((rows, width), f32)]
        + landed
        + landed[levels:]
        + [pltpu.SemaphoreType.DMA((len(pairs),))] * 2
        + [pltpu.SemaphoreType.DMA],
        compiler_params=pltpu.CompilerParams(
            collective_id=1 if doublings else 0,
            has_side_effects=True,
            vmem_limit_bytes=60 * 2**20,
        ),
        name="careful" if doublings else "tree",
    )(coupling, solved, *blocks)


def per_device(leaf_blocks, bases, targets, coupling):
    levels, rank = coupling.shape
    rows, size = leaf_blocks.shape
    right = targets.shape[1]
    width = right + rank * levels
    inner_bits = lax.axis_size("inner").bit_length() - 1
    f32 = jnp.float32
    widths = [width - rank * level for level in range(levels)]
    solved, *blocks = pl.pallas_call(
        functools.partial(leaf_kernel, rank, levels),
        out_shape=[jax.ShapeDtypeStruct((rows, width), f32)]
        + [jax.ShapeDtypeStruct((rank, wide), f32) for wide in widths],
        in_specs=[VMEM] * 3,
        out_specs=[VMEM] * (1 + levels),
        scratch_shapes=[pltpu.VMEM((2 * size, size), f32)],
        compiler_params=pltpu.CompilerParams(vmem_limit_bytes=60 * 2**20),
        name="leaf",
    )(leaf_blocks, bases.T, targets)
    worst = rank * (4.0 * rows * 2**levels / EIGEN_MIN + 1.0)
    doublings = math.ceil(math.log2(math.sqrt(worst) * 4.1))
    quick, flag = call_tree(coupling, solved, blocks, inner_bits, 0)
    return lax.cond(
        flag[0, 0] <= RESIDUAL_MAX,
        lambda: quick,
        lambda: call_tree(coupling, solved, blocks, inner_bits, doublings)[0],
    )


def solution(mesh):
    rows = P(("group", "inner"), None)
    return jax.shard_map(
        per_device,
        mesh=mesh,
        in_specs=(rows, rows, rows, P()),
        out_specs=rows,
        check_vma=False,
    )
```

```python
import functools
import math

import jax
import jax.numpy as jnp
from jax import lax
from jax.experimental import pallas as pl
from jax.experimental.pallas import tpu as pltpu
from jax.sharding import PartitionSpec as P

EIGEN_MIN = 0.4
LEAF_TOL = 3e-4
RESIDUAL_MAX = 1e-3
FLAG_ROWS = 8
RELAX = 1.5
VMEM = pl.BlockSpec(memory_space=pltpu.VMEM)


def mm(first, second):
    return jnp.dot(
        first,
        second,
        precision=lax.Precision.HIGHEST,
        preferred_element_type=jnp.float32,
    )


def split(value):
    high = value.astype(jnp.bfloat16)
    return high, (value - high.astype(jnp.float32)).astype(jnp.bfloat16)


def mm3(first, second):
    (a_high, a_low), (b_high, b_low) = split(first), split(second)
    dot = functools.partial(jnp.dot, preferred_element_type=jnp.float32)
    return dot(a_high, b_high) + (dot(a_high, b_low) + dot(a_low, b_high))


def mm_t(first, second):
    return lax.dot_general(
        first,
        second,
        (((0,), (0,)), ((), ())),
        precision=lax.Precision.HIGHEST,
        preferred_element_type=jnp.float32,
    )


def identity(size):
    rows = lax.broadcasted_iota(jnp.int32, (size, size), 0)
    cols = lax.broadcasted_iota(jnp.int32, (size, size), 1)
    return jnp.where(rows == cols, 1.0, 0.0).astype(jnp.float32)


def spd_solve(matrix, rhs, low, high, pair_ref):
    size = matrix.shape[0]
    eye = identity(size)
    alpha = 2.0 / (low + high)
    pair_ref[:size, :] = eye - alpha * matrix
    pair_ref[size:, :] = alpha * eye

    def cond(rho):
        return rho > LEAF_TOL

    def body(rho):
        square = rho * rho
        scale = 2.0 / (2.0 - square)
        pair = pair_ref[...]
        product = mm3(pair, pair[:size])
        pair_ref[:size, :] = (1.0 - scale) * eye + scale * product[:size]
        pair_ref[size:, :] = scale * (pair[size:] + product[size:])
        return square / (2.0 - square)

    lax.while_loop(cond, body, (high - low) / (high + low))

    @pl.when(high > 100.0 * low)
    def _():
        for _ in range(2):
            inverse = pair_ref[size:, :]
            pair_ref[size:, :] = inverse + mm(inverse, eye - mm(matrix, inverse))

    both = mm(pair_ref[size:, :], jnp.concatenate([matrix, rhs], axis=1))
    found = both[:, size:]
    return found + mm3(eye - both[:, :size], found)


def leaf_kernel(rank, levels, leaf_ref, bases_ref, targets_ref, solved_ref, *rest):
    blocks, pair_ref = rest[:levels], rest[levels]
    matrix = leaf_ref[...]
    high = jnp.max(jnp.sum(jnp.abs(matrix), axis=0, keepdims=True))
    flipped = jnp.concatenate(
        [
            bases_ref[rank * level : rank * (level + 1), :]
            for level in reversed(range(levels))
        ],
        axis=0,
    )
    rhs = jnp.concatenate([targets_ref[...], flipped.T], axis=1)
    high = jnp.maximum(high, 2 * EIGEN_MIN)
    solved = spd_solve(matrix, rhs, EIGEN_MIN, high, pair_ref)
    solved_ref[...] = solved
    gram = mm(bases_ref[...], solved)
    for level in range(levels):
        width = solved.shape[1] - rank * level
        blocks[level][...] = gram[rank * level : rank * (level + 1), :width]


def fixed_inverse(matrix, low, high, doublings):
    size = matrix.shape[0]
    eye = identity(size)
    alpha = 2.0 / (low + high)
    rho = (high - low) / (high + low)
    residual = eye - alpha * matrix
    inverse = alpha * eye
    for _ in range(doublings):
        square = rho * rho
        scale = 2.0 / (2.0 - square)
        rho = square / (2.0 - square)
        product = mm(jnp.concatenate([residual, inverse], axis=0), residual)
        inverse = scale * (inverse + product[size:])
        residual = (1.0 - scale) * eye + scale * product[:size]
    return inverse + mm(inverse, eye - mm(matrix, inverse))


def quick_solve(matrix, rhs):
    size = matrix.shape[0]
    eye = identity(size)
    residual = eye - matrix * (
        RELAX / jnp.sum(jnp.abs(matrix), axis=0, keepdims=True)
    )
    inverse = eye * (RELAX / jnp.sum(jnp.abs(matrix), axis=0, keepdims=True))
    for _ in range(3):
        product = mm3(jnp.concatenate([residual, inverse], axis=0), residual)
        inverse = inverse + product[size:]
        residual = product[:size]
    inverse = inverse + mm3(inverse, residual)
    both = mm(inverse, jnp.concatenate([rhs, matrix], axis=1))
    found = both[:, : rhs.shape[1]]
    error = eye - both[:, rhs.shape[1] :]
    worst = jnp.max(jnp.sum(jnp.abs(error), axis=0, keepdims=True))
    return found + mm3(error, found), worst


def capacity_solve(front, weights, rank, doublings):
    width = front.shape[1] - rank
    eye = identity(rank)
    extra = 1.0 / weights
    capacity = front[:, width:] + eye * extra
    if not doublings:
        return quick_solve(capacity, front[:, :width])
    diag_row = jnp.sum(capacity * eye, axis=0, keepdims=True)
    diag_col = jnp.sum(capacity * eye, axis=1, keepdims=True)
    root_row, root_col = lax.rsqrt(diag_row), lax.rsqrt(diag_col)
    scaled = 0.5 * (capacity + capacity.T) * root_row * root_col
    sums = jnp.sum(jnp.abs(scaled), axis=0, keepdims=True)
    high = jnp.broadcast_to(jnp.max(sums, axis=1, keepdims=True), (1, rank))
    low = 0.99 * jnp.min(extra / diag_row, axis=1, keepdims=True)
    low = jnp.broadcast_to(low, (1, rank))
    rhs = root_col * front[:, :width]
    return root_col * mm(fixed_inverse(scaled, low, high, doublings), rhs), None


def tree_kernel(rank, levels, inner_bits, doublings, coupling_ref, solved_ref, *refs):
    pairs = [(k, j) for k in range(levels) for j in range(k, levels)]
    number = {pair: index for index, pair in enumerate(pairs)}
    first, refs = refs[:levels], refs[levels:]
    if doublings:
        (rest_ref, coef_ref, state_ref), refs = refs[:3], refs[3:]
    else:
        (rest_ref, coef_ref, flag_ref, state_ref), refs = refs[:4], refs[4:]
    landed = dict(zip(pairs, refs[: len(pairs)]))
    later = pairs[levels:]
    own = dict(zip(pairs[:levels], first))
    own.update(zip(later, refs[len(pairs) : len(pairs) + len(later)]))
    weights_ref, send_sem, recv_sem, load_sem = refs[-4:]
    load = pltpu.make_async_copy(solved_ref, state_ref, load_sem.at[0])
    load_weights = pltpu.make_async_copy(coupling_ref, weights_ref, load_sem.at[1])
    load_weights.start()
    load.start()

    group, inner = lax.axis_index("group"), lax.axis_index("inner")

    def partner(level):
        if level < inner_bits:
            mask = 2**level
            return (group, inner + mask * (1 - 2 * ((inner // mask) % 2)))
        mask = 2 ** (level - inner_bits)
        return (group + mask * (1 - 2 * ((group // mask) % 2)), inner)

    partners = [partner(level) for level in range(levels)]

    def copy_of(k, j):
        return pltpu.make_async_remote_copy(
            src_ref=own[k, j],
            dst_ref=landed[k, j],
            send_sem=send_sem.at[number[k, j]],
            recv_sem=recv_sem.at[number[k, j]],
            device_id=partners[k],
            device_id_type=pl.DeviceIdType.MESH,
        )

    barrier = pltpu.get_barrier_semaphore()
    for other in partners:
        pl.semaphore_signal(
            barrier, inc=1, device_id=other, device_id_type=pl.DeviceIdType.MESH
        )
    pl.semaphore_wait(barrier, levels)

    for j in range(levels):
        copy_of(0, j).start()
    load_weights.wait()
    bad = 0.0
    for k in range(levels):
        copy_of(k, k).wait_recv()
        front = own[k, k][:rank, :] + landed[k, k][:rank, :]
        wide = front.shape[1] - rank
        coef, worst = capacity_solve(
            front, weights_ref[k : k + 1, :], rank, doublings
        )
        if not doublings:
            if k > 0:
                flags = jnp.maximum(own[k, k][rank:, :128], landed[k, k][rank:, :128])
                bad = jnp.max(flags)
            bad = jnp.maximum(bad, worst)
        if k + 1 < levels:
            base = wide - rank * (levels - 1 - k)
            update = mm_t(front[:, base:wide], coef)
            for j in range(k + 1, levels):
                rows = rank * (levels - 1 - j)
                columns = own[k, j].shape[1]
                copy_of(k, j).wait_recv()
                own[k + 1, j][:rank, :] = (own[k, j][...] + landed[k, j][...]) - update[
                    rows : rows + rank, :columns
                ]
                if j == k + 1 and not doublings:
                    own[k + 1, j][rank:, :] = jnp.full(
                        (FLAG_ROWS, columns), bad, jnp.float32
                    )
                copy_of(k + 1, j).start()
            if k == 0:
                load.wait()
            target = rest_ref if k + 2 == levels else state_ref
            target[:, :wide] = state_ref[:, :wide] - mm(
                state_ref[:, wide : wide + rank], coef
            )
        else:
            coef_ref[...] = coef
    if not doublings:
        flag_ref[0] = bad
    for pair in pairs:
        copy_of(*pair).wait_send()


def call_tree(coupling, solved, blocks, inner_bits, doublings):
    levels, rank = coupling.shape
    rows, width = solved.shape
    right = width - rank * levels
    f32 = jnp.float32
    pairs = [(k, j) for k in range(levels) for j in range(k, levels)]
    extra = 0 if doublings else FLAG_ROWS
    landed = [
        pltpu.VMEM((rank + (extra if j == k > 0 else 0), width - rank * j), f32)
        for k, j in pairs
    ]
    result = [
        jax.ShapeDtypeStruct((rows, right + rank), f32),
        jax.ShapeDtypeStruct((rank, right), f32),
    ]
    if not doublings:
        result.append(jax.ShapeDtypeStruct((1,), f32))
    return pl.pallas_call(
        functools.partial(tree_kernel, rank, levels, inner_bits, doublings),
        out_shape=result,
        in_specs=[pl.BlockSpec(memory_space=pl.ANY)] * 2 + [VMEM] * levels,
        out_specs=[VMEM] * 2 + [pl.BlockSpec(memory_space=pltpu.SMEM)] * (len(result) - 2),
        scratch_shapes=[pltpu.VMEM((rows, width), f32)]
        + landed
        + landed[levels:]
        + [pltpu.VMEM((levels, rank), f32)]
        + [pltpu.SemaphoreType.DMA((len(pairs),))] * 2
        + [pltpu.SemaphoreType.DMA((2,))],
        compiler_params=pltpu.CompilerParams(
            collective_id=1 if doublings else 0,
            has_side_effects=True,
            vmem_limit_bytes=60 * 2**20,
        ),
        name="careful" if doublings else "tree",
    )(coupling, solved, *blocks)


def last_kernel(rest_ref, coef_ref, out_ref):
    width = out_ref.shape[1]
    out_ref[...] = rest_ref[:, :width] - mm(rest_ref[:, width:], coef_ref[...])


def last_update(rest, coef):
    return pl.pallas_call(
        last_kernel,
        out_shape=jax.ShapeDtypeStruct((rest.shape[0], coef.shape[1]), jnp.float32),
        in_specs=[VMEM] * 2,
        out_specs=VMEM,
        name="last",
    )(rest, coef)


def per_device(leaf_blocks, bases, targets, coupling):
    levels, rank = coupling.shape
    rows, size = leaf_blocks.shape
    right = targets.shape[1]
    width = right + rank * levels
    inner_bits = lax.axis_size("inner").bit_length() - 1
    f32 = jnp.float32
    widths = [width - rank * level for level in range(levels)]
    solved, *blocks = pl.pallas_call(
        functools.partial(leaf_kernel, rank, levels),
        out_shape=[jax.ShapeDtypeStruct((rows, width), f32)]
        + [jax.ShapeDtypeStruct((rank, wide), f32) for wide in widths],
        in_specs=[VMEM] * 3,
        out_specs=[VMEM] * (1 + levels),
        scratch_shapes=[pltpu.VMEM((2 * size, size), f32)],
        compiler_params=pltpu.CompilerParams(vmem_limit_bytes=60 * 2**20),
        name="leaf",
    )(leaf_blocks, bases.T, targets)
    worst = rank * (4.0 * rows * 2**levels / EIGEN_MIN + 1.0)
    doublings = math.ceil(math.log2(math.sqrt(worst) * 4.1))
    rest, coef, flag = call_tree(coupling, solved, blocks, inner_bits, 0)

    def careful():
        return last_update(*call_tree(coupling, solved, blocks, inner_bits, doublings))

    return lax.cond(
        flag[0] <= RESIDUAL_MAX, lambda: last_update(rest, coef), careful
    )


def solution(mesh):
    rows = P(("group", "inner"), None)
    return jax.shard_map(
        per_device,
        mesh=mesh,
        in_specs=(rows, rows, rows, P()),
        out_specs=rows,
        check_vma=False,
    )
```

```python
import functools
import math

import jax
import jax.numpy as jnp
from jax import lax
from jax.experimental import pallas as pl
from jax.experimental.pallas import tpu as pltpu
from jax.sharding import PartitionSpec as P

EIGEN_MIN = 0.4
LEAF_TOL = 3e-4
RESIDUAL_MAX = 1e-3
FLAG_ROWS = 8
RELAX = 1.5
VMEM = pl.BlockSpec(memory_space=pltpu.VMEM)


def mm(first, second):
    return jnp.dot(
        first,
        second,
        precision=lax.Precision.HIGHEST,
        preferred_element_type=jnp.float32,
    )


def split(value):
    high = value.astype(jnp.bfloat16)
    return high, (value - high.astype(jnp.float32)).astype(jnp.bfloat16)


def mm3(first, second):
    (a_high, a_low), (b_high, b_low) = split(first), split(second)
    dot = functools.partial(jnp.dot, preferred_element_type=jnp.float32)
    return dot(a_high, b_high) + (dot(a_high, b_low) + dot(a_low, b_high))


def mm_t(first, second):
    return lax.dot_general(
        first,
        second,
        (((0,), (0,)), ((), ())),
        precision=lax.Precision.HIGHEST,
        preferred_element_type=jnp.float32,
    )


def identity(size):
    rows = lax.broadcasted_iota(jnp.int32, (size, size), 0)
    cols = lax.broadcasted_iota(jnp.int32, (size, size), 1)
    return jnp.where(rows == cols, 1.0, 0.0).astype(jnp.float32)


def spd_solve(matrix, rhs, low, high, pair_ref):
    size = matrix.shape[0]
    eye = identity(size)
    alpha = 2.0 / (low + high)
    pair_ref[:size, :] = eye - alpha * matrix
    pair_ref[size:, :] = alpha * eye

    def cond(rho):
        return rho > LEAF_TOL

    def body(rho):
        square = rho * rho
        scale = 2.0 / (2.0 - square)
        pair = pair_ref[...]
        product = mm3(pair, pair[:size])
        pair_ref[:size, :] = (1.0 - scale) * eye + scale * product[:size]
        pair_ref[size:, :] = scale * (pair[size:] + product[size:])
        return square / (2.0 - square)

    lax.while_loop(cond, body, (high - low) / (high + low))

    @pl.when(high > 100.0 * low)
    def _():
        for _ in range(2):
            inverse = pair_ref[size:, :]
            pair_ref[size:, :] = inverse + mm(inverse, eye - mm(matrix, inverse))

    both = mm(pair_ref[size:, :], jnp.concatenate([matrix, rhs], axis=1))
    found = both[:, size:]
    return found + mm3(eye - both[:, :size], found)


def leaf_kernel(rank, levels, leaf_ref, bases_ref, targets_ref, coupling_ref, *rest):
    solved_ref, extra_ref, rest = rest[0], rest[1], rest[2:]
    blocks, pair_ref = rest[:levels], rest[levels]
    extra_ref[...] = 1.0 / coupling_ref[...]
    matrix = leaf_ref[...]
    high = jnp.max(jnp.sum(jnp.abs(matrix), axis=0, keepdims=True))
    flipped = jnp.concatenate(
        [
            bases_ref[rank * level : rank * (level + 1), :]
            for level in reversed(range(levels))
        ],
        axis=0,
    )
    rhs = jnp.concatenate([targets_ref[...], flipped.T], axis=1)
    high = jnp.maximum(high, 2 * EIGEN_MIN)
    solved = spd_solve(matrix, rhs, EIGEN_MIN, high, pair_ref)
    solved_ref[...] = solved
    gram = mm(bases_ref[...], solved)
    for level in range(levels):
        width = solved.shape[1] - rank * level
        blocks[level][...] = gram[rank * level : rank * (level + 1), :width]


def fixed_inverse(matrix, low, high, doublings):
    size = matrix.shape[0]
    eye = identity(size)
    alpha = 2.0 / (low + high)
    rho = (high - low) / (high + low)
    residual = eye - alpha * matrix
    inverse = alpha * eye
    for _ in range(doublings):
        square = rho * rho
        scale = 2.0 / (2.0 - square)
        rho = square / (2.0 - square)
        product = mm(jnp.concatenate([residual, inverse], axis=0), residual)
        inverse = scale * (inverse + product[size:])
        residual = (1.0 - scale) * eye + scale * product[:size]
    return inverse + mm(inverse, eye - mm(matrix, inverse))


def quick_solve(matrix, rhs, between):
    size = matrix.shape[0]
    eye = identity(size)
    residual = eye - matrix * (
        RELAX / jnp.sum(jnp.abs(matrix), axis=0, keepdims=True)
    )
    inverse = eye * (RELAX / jnp.sum(jnp.abs(matrix), axis=0, keepdims=True))
    for _ in range(3):
        product = mm3(jnp.concatenate([residual, inverse], axis=0), residual)
        inverse = inverse + product[size:]
        residual = product[:size]
    inverse = inverse + mm3(inverse, residual)
    between()
    both = mm(inverse, jnp.concatenate([rhs, matrix], axis=1))
    found = both[:, : rhs.shape[1]]
    error = eye - both[:, rhs.shape[1] :]
    worst = jnp.sum(jnp.abs(error), axis=0, keepdims=True)
    return found + mm3(error, found), worst


def capacity_solve(front, extra, rank, doublings, between):
    width = front.shape[1] - rank
    eye = identity(rank)
    capacity = front[:, width:] + eye * extra
    if not doublings:
        return quick_solve(capacity, front[:, :width], between)
    between()
    diag_row = jnp.sum(capacity * eye, axis=0, keepdims=True)
    diag_col = jnp.sum(capacity * eye, axis=1, keepdims=True)
    root_row, root_col = lax.rsqrt(diag_row), lax.rsqrt(diag_col)
    scaled = 0.5 * (capacity + capacity.T) * root_row * root_col
    sums = jnp.sum(jnp.abs(scaled), axis=0, keepdims=True)
    high = jnp.broadcast_to(jnp.max(sums, axis=1, keepdims=True), (1, rank))
    low = 0.99 * jnp.min(extra / diag_row, axis=1, keepdims=True)
    low = jnp.broadcast_to(low, (1, rank))
    rhs = root_col * front[:, :width]
    return root_col * mm(fixed_inverse(scaled, low, high, doublings), rhs), None


def tree_kernel(rank, levels, inner_bits, doublings, extra_ref, solved_ref, *refs):
    pairs = [(k, j) for k in range(levels) for j in range(k, levels)]
    number = {pair: index for index, pair in enumerate(pairs)}
    first, refs = refs[:levels], refs[levels:]
    if doublings:
        (rest_ref, coef_ref, state_ref), refs = refs[:3], refs[3:]
    else:
        (rest_ref, coef_ref, flag_ref, state_ref), refs = refs[:4], refs[4:]
    landed = dict(zip(pairs, refs[: len(pairs)]))
    later = pairs[levels:]
    own = dict(zip(pairs[:levels], first))
    own.update(zip(later, refs[len(pairs) : len(pairs) + len(later)]))
    send_sem, recv_sem, load_sem = refs[-3:]
    load = pltpu.make_async_copy(solved_ref, state_ref, load_sem)
    load.start()
    if not doublings:
        for k in range(1, levels):
            own[k, k][rank:, :] = jnp.zeros((FLAG_ROWS, own[k, k].shape[1]), jnp.float32)

    group, inner = lax.axis_index("group"), lax.axis_index("inner")

    def partner(level):
        if level < inner_bits:
            mask = 2**level
            return (group, inner + mask * (1 - 2 * ((inner // mask) % 2)))
        mask = 2 ** (level - inner_bits)
        return (group + mask * (1 - 2 * ((group // mask) % 2)), inner)

    partners = [partner(level) for level in range(levels)]

    def copy_of(k, j):
        return pltpu.make_async_remote_copy(
            src_ref=own[k, j],
            dst_ref=landed[k, j],
            send_sem=send_sem.at[number[k, j]],
            recv_sem=recv_sem.at[number[k, j]],
            device_id=partners[k],
            device_id_type=pl.DeviceIdType.MESH,
        )

    barrier = pltpu.get_barrier_semaphore()
    for other in partners:
        pl.semaphore_signal(
            barrier, inc=1, device_id=other, device_id_type=pl.DeviceIdType.MESH
        )
    pl.semaphore_wait(barrier, levels)

    sent = []

    def send(k, j):
        if (k, j - 1) in pairs:
            copy_of(k, j - 1).wait_send()
            sent.append((k, j - 1))
        copy_of(k, j).start()

    def send_first(j):
        if j < levels:
            send(0, j)

    send_first(0)
    send_first(1)
    bad = jnp.zeros((1, rank), jnp.float32)
    for k in range(levels):
        copy_of(k, k).wait_recv()
        front = own[k, k][:rank, :] + landed[k, k][:rank, :]
        wide = front.shape[1] - rank
        base = wide - rank * (levels - 1 - k)
        turned = front[:, base:wide].T if k + 1 < levels else None
        coef, worst = capacity_solve(
            front,
            extra_ref[k : k + 1, :],
            rank,
            doublings,
            lambda: send_first(2) if k == 0 else None,
        )
        if not doublings:
            if k > 0:
                flags = jnp.maximum(own[k, k][rank:, :rank], landed[k, k][rank:, :rank])
                bad = jnp.maximum(bad, flags[:1, :])
            bad = jnp.maximum(bad, worst)
        if k + 1 == levels:
            coef_ref[...] = coef
        for j in range(k + 1, levels):
            rows = rank * (levels - 1 - j)
            columns = own[k, j].shape[1]
            update = mm(turned[rows : rows + rank, :], coef[:, :columns])
            copy_of(k, j).wait_recv()
            own[k + 1, j][:rank, :] = own[k, j][...] + landed[k, j][...] - update
            if j == k + 1 and not doublings:
                own[k + 1, j][rank:, :rank] = jnp.broadcast_to(bad, (FLAG_ROWS, rank))
            send(k + 1, j)
            if k == 0:
                send_first(j + 2)
            if j == k + 1:
                if k == 0:
                    load.wait()
                target = rest_ref if k + 2 == levels else state_ref
                target[:, :wide] = state_ref[:, :wide] - mm(
                    state_ref[:, wide : wide + rank], coef
                )
    if not doublings:
        flag_ref[0] = jnp.max(bad)
    for pair in pairs:
        if pair not in sent:
            copy_of(*pair).wait_send()


def call_tree(extra, solved, blocks, inner_bits, doublings):
    levels, rank = extra.shape
    rows, width = solved.shape
    right = width - rank * levels
    f32 = jnp.float32
    pairs = [(k, j) for k in range(levels) for j in range(k, levels)]
    flag_rows = 0 if doublings else FLAG_ROWS
    landed = [
        pltpu.VMEM((rank + (flag_rows if j == k > 0 else 0), width - rank * j), f32)
        for k, j in pairs
    ]
    result = [
        jax.ShapeDtypeStruct((rows, right + rank), f32),
        jax.ShapeDtypeStruct((rank, right), f32),
    ]
    if not doublings:
        result.append(jax.ShapeDtypeStruct((1,), f32))
    return pl.pallas_call(
        functools.partial(tree_kernel, rank, levels, inner_bits, doublings),
        out_shape=result,
        in_specs=[VMEM, pl.BlockSpec(memory_space=pl.ANY)] + [VMEM] * levels,
        out_specs=[VMEM] * 2 + [pl.BlockSpec(memory_space=pltpu.SMEM)] * (len(result) - 2),
        scratch_shapes=[pltpu.VMEM((rows, width), f32)]
        + landed
        + landed[levels:]
        + [pltpu.SemaphoreType.DMA((len(pairs),))] * 2
        + [pltpu.SemaphoreType.DMA],
        compiler_params=pltpu.CompilerParams(
            collective_id=1 if doublings else 0,
            has_side_effects=True,
            vmem_limit_bytes=60 * 2**20,
        ),
        name="careful" if doublings else "tree",
    )(extra, solved, *blocks)


def last_kernel(rest_ref, coef_ref, out_ref):
    width = out_ref.shape[1]
    out_ref[...] = rest_ref[:, :width] - mm(rest_ref[:, width:], coef_ref[...])


def last_update(rest, coef):
    return pl.pallas_call(
        last_kernel,
        out_shape=jax.ShapeDtypeStruct((rest.shape[0], coef.shape[1]), jnp.float32),
        in_specs=[VMEM] * 2,
        out_specs=VMEM,
        compiler_params=pltpu.CompilerParams(vmem_limit_bytes=60 * 2**20),
        name="last",
    )(rest, coef)


def per_device(leaf_blocks, bases, targets, coupling):
    levels, rank = coupling.shape
    rows, size = leaf_blocks.shape
    right = targets.shape[1]
    width = right + rank * levels
    inner_bits = lax.axis_size("inner").bit_length() - 1
    f32 = jnp.float32
    widths = [width - rank * level for level in range(levels)]
    solved, extra, *blocks = pl.pallas_call(
        functools.partial(leaf_kernel, rank, levels),
        out_shape=[
            jax.ShapeDtypeStruct((rows, width), f32),
            jax.ShapeDtypeStruct((levels, rank), f32),
        ]
        + [jax.ShapeDtypeStruct((rank, wide), f32) for wide in widths],
        in_specs=[VMEM] * 4,
        out_specs=[VMEM] * (2 + levels),
        scratch_shapes=[pltpu.VMEM((2 * size, size), f32)],
        compiler_params=pltpu.CompilerParams(vmem_limit_bytes=60 * 2**20),
        name="leaf",
    )(leaf_blocks, bases.T, targets, coupling)
    worst = rank * (4.0 * rows * 2**levels / EIGEN_MIN + 1.0)
    doublings = math.ceil(math.log2(math.sqrt(worst) * 4.1))
    rest, coef, flag = call_tree(extra, solved, blocks, inner_bits, 0)

    def careful():
        return last_update(*call_tree(extra, solved, blocks, inner_bits, doublings))

    return lax.cond(
        flag[0] <= RESIDUAL_MAX, lambda: last_update(rest, coef), careful
    )


def solution(mesh):
    rows = P(("group", "inner"), None)
    return jax.shard_map(
        per_device,
        mesh=mesh,
        in_specs=(rows, rows, rows, P()),
        out_specs=rows,
        check_vma=False,
    )
```

```python
import functools
import math

import jax
import jax.numpy as jnp
from jax import lax
from jax.experimental import pallas as pl
from jax.experimental.pallas import tpu as pltpu
from jax.sharding import PartitionSpec as P

EIGEN_MIN = 0.4
LEAF_TOL = 3e-4
RESIDUAL_MAX = 1e-3
FLAG_ROWS = 8
RELAX = 1.5
LANES = 128
VMEM = pl.BlockSpec(memory_space=pltpu.VMEM)


def mm(first, second):
    return jnp.dot(
        first,
        second,
        precision=lax.Precision.HIGHEST,
        preferred_element_type=jnp.float32,
    )


def split(value):
    high = value.astype(jnp.bfloat16)
    return high, (value - high.astype(jnp.float32)).astype(jnp.bfloat16)


def mm3(first, second):
    (a_high, a_low), (b_high, b_low) = split(first), split(second)
    dot = functools.partial(jnp.dot, preferred_element_type=jnp.float32)
    return dot(a_high, b_high) + (dot(a_high, b_low) + dot(a_low, b_high))


def mm_t(first, second):
    return lax.dot_general(
        first,
        second,
        (((0,), (0,)), ((), ())),
        precision=lax.Precision.HIGHEST,
        preferred_element_type=jnp.float32,
    )


def packed_rows(rank, width):
    return rank * (width // LANES) + (rank // 2 if width % LANES else 0)


def pack(value):
    rank, width = value.shape
    full = width // LANES
    tiles = [value[:, LANES * t : LANES * (t + 1)] for t in range(full)]
    if width % LANES:
        tail = value[:, LANES * full :]
        tiles.append(jnp.concatenate([tail[: rank // 2], tail[rank // 2 :]], axis=1))
    return jnp.concatenate(tiles, axis=0)


def unpack(value, rank, width):
    full = width // LANES
    tiles = [value[rank * t : rank * (t + 1), :] for t in range(full)]
    if width % LANES:
        tail = value[rank * full :, :]
        half = LANES // 2
        tiles.append(jnp.concatenate([tail[:, :half], tail[:, half:]], axis=0))
    return jnp.concatenate(tiles, axis=1)


def identity(size):
    rows = lax.broadcasted_iota(jnp.int32, (size, size), 0)
    cols = lax.broadcasted_iota(jnp.int32, (size, size), 1)
    return jnp.where(rows == cols, 1.0, 0.0).astype(jnp.float32)


def spd_solve(matrix, rhs, low, high, pair_ref):
    size = matrix.shape[0]
    eye = identity(size)
    alpha = 2.0 / (low + high)
    pair_ref[:size, :] = eye - alpha * matrix
    pair_ref[size:, :] = alpha * eye

    def cond(rho):
        return rho > LEAF_TOL

    def body(rho):
        square = rho * rho
        scale = 2.0 / (2.0 - square)
        pair = pair_ref[...]
        product = mm3(pair, pair[:size])
        pair_ref[:size, :] = (1.0 - scale) * eye + scale * product[:size]
        pair_ref[size:, :] = scale * (pair[size:] + product[size:])
        return square / (2.0 - square)

    lax.while_loop(cond, body, (high - low) / (high + low))

    @pl.when(high > 100.0 * low)
    def _():
        for _ in range(2):
            inverse = pair_ref[size:, :]
            pair_ref[size:, :] = inverse + mm(inverse, eye - mm(matrix, inverse))

    both = mm(pair_ref[size:, :], jnp.concatenate([matrix, rhs], axis=1))
    found = both[:, size:]
    return found + mm3(eye - both[:, :size], found)


def leaf_kernel(rank, levels, leaf_ref, bases_ref, targets_ref, coupling_ref, *rest):
    solved_ref, extra_ref, rest = rest[0], rest[1], rest[2:]
    blocks, pair_ref = rest[:levels], rest[levels]
    extra_ref[...] = 1.0 / coupling_ref[...]
    matrix = leaf_ref[...]
    high = jnp.max(jnp.sum(jnp.abs(matrix), axis=0, keepdims=True))
    flipped = jnp.concatenate(
        [
            bases_ref[rank * level : rank * (level + 1), :]
            for level in reversed(range(levels))
        ],
        axis=0,
    )
    rhs = jnp.concatenate([targets_ref[...], flipped.T], axis=1)
    high = jnp.maximum(high, 2 * EIGEN_MIN)
    solved = spd_solve(matrix, rhs, EIGEN_MIN, high, pair_ref)
    solved_ref[...] = solved
    gram = mm(bases_ref[...], solved)
    for level in range(levels):
        width = solved.shape[1] - rank * level
        blocks[level][...] = pack(gram[rank * level : rank * (level + 1), :width])


def fixed_inverse(matrix, low, high, doublings):
    size = matrix.shape[0]
    eye = identity(size)
    alpha = 2.0 / (low + high)
    rho = (high - low) / (high + low)
    residual = eye - alpha * matrix
    inverse = alpha * eye
    for _ in range(doublings):
        square = rho * rho
        scale = 2.0 / (2.0 - square)
        rho = square / (2.0 - square)
        product = mm(jnp.concatenate([residual, inverse], axis=0), residual)
        inverse = scale * (inverse + product[size:])
        residual = (1.0 - scale) * eye + scale * product[:size]
    return inverse + mm(inverse, eye - mm(matrix, inverse))


def quick_solve(matrix, rhs, squarings):
    size = matrix.shape[0]
    eye = identity(size)
    residual = eye - matrix * (
        RELAX / jnp.sum(jnp.abs(matrix), axis=0, keepdims=True)
    )
    inverse = eye * (RELAX / jnp.sum(jnp.abs(matrix), axis=0, keepdims=True))
    for _ in range(squarings - 1):
        product = mm3(jnp.concatenate([residual, inverse], axis=0), residual)
        inverse = inverse + product[size:]
        residual = product[:size]
    inverse = inverse + mm3(inverse, residual)
    both = mm(inverse, jnp.concatenate([rhs, matrix], axis=1))
    found = both[:, : rhs.shape[1]]
    error = eye - both[:, rhs.shape[1] :]
    worst = jnp.sum(jnp.abs(error), axis=0, keepdims=True)
    return found + mm3(error, found), worst


def capacity_solve(front, extra, rank, doublings, squarings):
    width = front.shape[1] - rank
    eye = identity(rank)
    capacity = front[:, width:] + eye * extra
    if not doublings:
        return quick_solve(capacity, front[:, :width], squarings)
    diag_row = jnp.sum(capacity * eye, axis=0, keepdims=True)
    diag_col = jnp.sum(capacity * eye, axis=1, keepdims=True)
    root_row, root_col = lax.rsqrt(diag_row), lax.rsqrt(diag_col)
    scaled = 0.5 * (capacity + capacity.T) * root_row * root_col
    sums = jnp.sum(jnp.abs(scaled), axis=0, keepdims=True)
    high = jnp.broadcast_to(jnp.max(sums, axis=1, keepdims=True), (1, rank))
    low = 0.99 * jnp.min(extra / diag_row, axis=1, keepdims=True)
    low = jnp.broadcast_to(low, (1, rank))
    rhs = root_col * front[:, :width]
    return root_col * mm(fixed_inverse(scaled, low, high, doublings), rhs), None


def tree_kernel(rank, levels, inner_bits, doublings, extra_ref, solved_ref, *refs):
    pairs = [(k, j) for k in range(levels) for j in range(k, levels)]
    number = {pair: index for index, pair in enumerate(pairs)}
    first, refs = refs[:levels], refs[levels:]
    if doublings:
        (rest_ref, coef_ref, state_ref), refs = refs[:3], refs[3:]
    else:
        (rest_ref, coef_ref, flag_ref, state_ref), refs = refs[:4], refs[4:]
    landed = dict(zip(pairs, refs[: len(pairs)]))
    later = pairs[levels:]
    own = dict(zip(pairs[:levels], first))
    own.update(zip(later, refs[len(pairs) : len(pairs) + len(later)]))
    send_sem, recv_sem, load_sem = refs[-3:]
    load = pltpu.make_async_copy(solved_ref, state_ref, load_sem)
    load.start()
    widths = [solved_ref.shape[1] - rank * j for j in range(levels)]
    heights = [packed_rows(rank, wide) for wide in widths]
    if not doublings:
        for k in range(1, levels):
            own[k, k][heights[k] :, :] = jnp.zeros((FLAG_ROWS, LANES), jnp.float32)

    group, inner = lax.axis_index("group"), lax.axis_index("inner")

    def partner(level):
        if level < inner_bits:
            mask = 2**level
            return (group, inner + mask * (1 - 2 * ((inner // mask) % 2)))
        mask = 2 ** (level - inner_bits)
        return (group + mask * (1 - 2 * ((group // mask) % 2)), inner)

    partners = [partner(level) for level in range(levels)]

    def copy_of(k, j):
        return pltpu.make_async_remote_copy(
            src_ref=own[k, j],
            dst_ref=landed[k, j],
            send_sem=send_sem.at[number[k, j]],
            recv_sem=recv_sem.at[number[k, j]],
            device_id=partners[k],
            device_id_type=pl.DeviceIdType.MESH,
        )

    barrier = pltpu.get_barrier_semaphore()
    for other in partners:
        pl.semaphore_signal(
            barrier, inc=1, device_id=other, device_id_type=pl.DeviceIdType.MESH
        )
    pl.semaphore_wait(barrier, levels)

    for j in range(levels):
        copy_of(0, j).start()
    bad = jnp.zeros((1, rank), jnp.float32)
    for k in range(levels):
        copy_of(k, k).wait_recv()
        height = heights[k]
        front = own[k, k][:height, :] + landed[k, k][:height, :]
        front = unpack(front, rank, widths[k])
        wide = front.shape[1] - rank
        base = wide - rank * (levels - 1 - k)
        turned = front[:, base:wide].T if k + 1 < levels else None
        coef, worst = capacity_solve(
            front,
            extra_ref[k : k + 1, :],
            rank,
            doublings,
            5 if k == 0 else 4,
        )
        if not doublings:
            if k > 0:
                flags = jnp.maximum(own[k, k][height:, :], landed[k, k][height:, :])
                bad = jnp.maximum(bad, flags[:1, :rank])
            bad = jnp.maximum(bad, worst)
        if k + 1 == levels:
            coef_ref[...] = coef
        for j in range(k + 1, levels):
            rows = rank * (levels - 1 - j)
            update = pack(mm(turned[rows : rows + rank, :], coef[:, : widths[j]]))
            copy_of(k, j).wait_recv()
            total = own[k, j][...] + landed[k, j][...] - update
            own[k + 1, j][: heights[j], :] = total
            if j == k + 1 and not doublings:
                own[k + 1, j][heights[j] :, :rank] = jnp.broadcast_to(
                    bad, (FLAG_ROWS, rank)
                )
            copy_of(k + 1, j).start()
            if j == k + 1:
                if k == 0:
                    load.wait()
                target = rest_ref if k + 2 == levels else state_ref
                target[:, :wide] = state_ref[:, :wide] - mm(
                    state_ref[:, wide : wide + rank], coef
                )
    if not doublings:
        flag_ref[0] = jnp.max(bad)
    for pair in pairs:
        copy_of(*pair).wait_send()


def call_tree(extra, solved, blocks, inner_bits, doublings):
    levels, rank = extra.shape
    rows, width = solved.shape
    right = width - rank * levels
    f32 = jnp.float32
    pairs = [(k, j) for k in range(levels) for j in range(k, levels)]
    flag_rows = 0 if doublings else FLAG_ROWS
    landed = [
        pltpu.VMEM(
            (
                packed_rows(rank, width - rank * j) + (flag_rows if j == k > 0 else 0),
                LANES,
            ),
            f32,
        )
        for k, j in pairs
    ]
    result = [
        jax.ShapeDtypeStruct((rows, right + rank), f32),
        jax.ShapeDtypeStruct((rank, right), f32),
    ]
    if not doublings:
        result.append(jax.ShapeDtypeStruct((1,), f32))
    return pl.pallas_call(
        functools.partial(tree_kernel, rank, levels, inner_bits, doublings),
        out_shape=result,
        in_specs=[VMEM, pl.BlockSpec(memory_space=pl.ANY)] + [VMEM] * levels,
        out_specs=[VMEM] * 2 + [pl.BlockSpec(memory_space=pltpu.SMEM)] * (len(result) - 2),
        scratch_shapes=[pltpu.VMEM((rows, width), f32)]
        + landed
        + landed[levels:]
        + [pltpu.SemaphoreType.DMA((len(pairs),))] * 2
        + [pltpu.SemaphoreType.DMA],
        compiler_params=pltpu.CompilerParams(
            collective_id=1 if doublings else 0,
            has_side_effects=True,
            vmem_limit_bytes=60 * 2**20,
        ),
        name="careful" if doublings else "tree",
    )(extra, solved, *blocks)


def last_kernel(rest_ref, coef_ref, out_ref):
    width = out_ref.shape[1]
    out_ref[...] = rest_ref[:, :width] - mm(rest_ref[:, width:], coef_ref[...])


def last_update(rest, coef):
    return pl.pallas_call(
        last_kernel,
        out_shape=jax.ShapeDtypeStruct((rest.shape[0], coef.shape[1]), jnp.float32),
        in_specs=[VMEM] * 2,
        out_specs=VMEM,
        compiler_params=pltpu.CompilerParams(vmem_limit_bytes=60 * 2**20),
        name="last",
    )(rest, coef)


def per_device(leaf_blocks, bases, targets, coupling):
    levels, rank = coupling.shape
    rows, size = leaf_blocks.shape
    right = targets.shape[1]
    width = right + rank * levels
    inner_bits = lax.axis_size("inner").bit_length() - 1
    f32 = jnp.float32
    widths = [width - rank * level for level in range(levels)]
    solved, extra, *blocks = pl.pallas_call(
        functools.partial(leaf_kernel, rank, levels),
        out_shape=[
            jax.ShapeDtypeStruct((rows, width), f32),
            jax.ShapeDtypeStruct((levels, rank), f32),
        ]
        + [jax.ShapeDtypeStruct((packed_rows(rank, wide), LANES), f32) for wide in widths],
        in_specs=[VMEM] * 4,
        out_specs=[VMEM] * (2 + levels),
        scratch_shapes=[pltpu.VMEM((2 * size, size), f32)],
        compiler_params=pltpu.CompilerParams(vmem_limit_bytes=60 * 2**20),
        name="leaf",
    )(leaf_blocks, bases.T, targets, coupling)
    worst = rank * (4.0 * rows * 2**levels / EIGEN_MIN + 1.0)
    doublings = math.ceil(math.log2(math.sqrt(worst) * 4.1))
    rest, coef, flag = call_tree(extra, solved, blocks, inner_bits, 0)

    def careful():
        return last_update(*call_tree(extra, solved, blocks, inner_bits, doublings))

    return lax.cond(
        flag[0] <= RESIDUAL_MAX, lambda: last_update(rest, coef), careful
    )


def solution(mesh):
    rows = P(("group", "inner"), None)
    return jax.shard_map(
        per_device,
        mesh=mesh,
        in_specs=(rows, rows, rows, P()),
        out_specs=rows,
        check_vma=False,
    )
```

```python
import functools
import math

import jax
import jax.numpy as jnp
from jax import lax
from jax.experimental import pallas as pl
from jax.experimental.pallas import tpu as pltpu
from jax.sharding import PartitionSpec as P

EIGEN_MIN = 0.4
LEAF_TOL = 3e-4
RESIDUAL_MAX = 1e-3
FLAG_ROWS = 8
RELAX = 1.5
LANES = 128
VMEM = pl.BlockSpec(memory_space=pltpu.VMEM)


def mm(first, second):
    return jnp.dot(
        first,
        second,
        precision=lax.Precision.HIGHEST,
        preferred_element_type=jnp.float32,
    )


def split(value):
    high = value.astype(jnp.bfloat16)
    return high, (value - high.astype(jnp.float32)).astype(jnp.bfloat16)


def mm3(first, second):
    (a_high, a_low), (b_high, b_low) = split(first), split(second)
    dot = functools.partial(jnp.dot, preferred_element_type=jnp.float32)
    return dot(a_high, b_high) + (dot(a_high, b_low) + dot(a_low, b_high))


def mm_t(first, second):
    return lax.dot_general(
        first,
        second,
        (((0,), (0,)), ((), ())),
        precision=lax.Precision.HIGHEST,
        preferred_element_type=jnp.float32,
    )


def packed_rows(rank, width):
    return rank * (width // LANES) + (rank // 2 if width % LANES else 0)


def pack(value):
    rank, width = value.shape
    full = width // LANES
    tiles = [value[:, LANES * t : LANES * (t + 1)] for t in range(full)]
    if width % LANES:
        tail = value[:, LANES * full :]
        tiles.append(jnp.concatenate([tail[: rank // 2], tail[rank // 2 :]], axis=1))
    return jnp.concatenate(tiles, axis=0)


def unpack(value, rank, width):
    full = width // LANES
    tiles = [value[rank * t : rank * (t + 1), :] for t in range(full)]
    if width % LANES:
        tail = value[rank * full :, :]
        half = LANES // 2
        tiles.append(jnp.concatenate([tail[:, :half], tail[:, half:]], axis=0))
    return jnp.concatenate(tiles, axis=1)


def identity(size):
    rows = lax.broadcasted_iota(jnp.int32, (size, size), 0)
    cols = lax.broadcasted_iota(jnp.int32, (size, size), 1)
    return jnp.where(rows == cols, 1.0, 0.0).astype(jnp.float32)


def spd_solve(matrix, rhs, low, high, pair_ref):
    size = matrix.shape[0]
    eye = identity(size)
    alpha = 2.0 / (low + high)
    rho = (high - low) / (high + low)
    scale = 2.0 / (2.0 - rho * rho)
    residual = eye - alpha * matrix
    pair_ref[:size, :] = (1.0 - scale) * eye + scale * mm3(residual, residual)
    pair_ref[size:, :] = (scale * alpha) * (eye + residual)

    def cond(rho):
        return rho > LEAF_TOL

    def body(rho):
        square = rho * rho
        scale = 2.0 / (2.0 - square)
        pair = pair_ref[...]
        product = mm3(pair, pair[:size])
        pair_ref[:size, :] = (1.0 - scale) * eye + scale * product[:size]
        pair_ref[size:, :] = scale * (pair[size:] + product[size:])
        return square / (2.0 - square)

    lax.while_loop(cond, body, rho * rho / (2.0 - rho * rho))

    @pl.when(high > 100.0 * low)
    def _():
        for _ in range(2):
            inverse = pair_ref[size:, :]
            pair_ref[size:, :] = inverse + mm(inverse, eye - mm(matrix, inverse))

    both = mm(pair_ref[size:, :], jnp.concatenate([matrix, rhs], axis=1))
    found = both[:, size:]
    return found + mm3(eye - both[:, :size], found)


def leaf_kernel(rank, levels, leaf_ref, bases_ref, targets_ref, coupling_ref, *rest):
    solved_ref, extra_ref, rest = rest[0], rest[1], rest[2:]
    blocks, pair_ref = rest[:levels], rest[levels]
    extra_ref[...] = 1.0 / coupling_ref[...]
    matrix = leaf_ref[...]
    high = jnp.max(jnp.sum(jnp.abs(matrix), axis=0, keepdims=True))
    flipped = jnp.concatenate(
        [
            bases_ref[rank * level : rank * (level + 1), :]
            for level in reversed(range(levels))
        ],
        axis=0,
    )
    rhs = jnp.concatenate([targets_ref[...], flipped.T], axis=1)
    high = jnp.maximum(high, 2 * EIGEN_MIN)
    solved = spd_solve(matrix, rhs, EIGEN_MIN, high, pair_ref)
    solved_ref[...] = solved
    gram = mm(bases_ref[...], solved)
    for level in range(levels):
        width = solved.shape[1] - rank * level
        blocks[level][...] = pack(gram[rank * level : rank * (level + 1), :width])


def fixed_inverse(matrix, low, high, doublings):
    size = matrix.shape[0]
    eye = identity(size)
    alpha = 2.0 / (low + high)
    rho = (high - low) / (high + low)
    residual = eye - alpha * matrix
    inverse = alpha * eye
    for _ in range(doublings):
        square = rho * rho
        scale = 2.0 / (2.0 - square)
        rho = square / (2.0 - square)
        product = mm(jnp.concatenate([residual, inverse], axis=0), residual)
        inverse = scale * (inverse + product[size:])
        residual = (1.0 - scale) * eye + scale * product[:size]
    return inverse + mm(inverse, eye - mm(matrix, inverse))


def quick_solve(matrix, rhs, squarings):
    size = matrix.shape[0]
    eye = identity(size)
    residual = eye - matrix * (
        RELAX / jnp.sum(jnp.abs(matrix), axis=0, keepdims=True)
    )
    inverse = eye * (RELAX / jnp.sum(jnp.abs(matrix), axis=0, keepdims=True))
    for _ in range(squarings - 1):
        product = mm3(jnp.concatenate([residual, inverse], axis=0), residual)
        inverse = inverse + product[size:]
        residual = product[:size]
    inverse = inverse + mm3(inverse, residual)
    both = mm(inverse, jnp.concatenate([rhs, matrix], axis=1))
    found = both[:, : rhs.shape[1]]
    error = eye - both[:, rhs.shape[1] :]
    worst = jnp.sum(jnp.abs(error), axis=0, keepdims=True)
    return found + mm3(error, found), worst


def capacity_solve(front, extra, rank, doublings, squarings):
    width = front.shape[1] - rank
    eye = identity(rank)
    capacity = front[:, width:] + eye * extra
    if not doublings:
        return quick_solve(capacity, front[:, :width], squarings)
    diag_row = jnp.sum(capacity * eye, axis=0, keepdims=True)
    diag_col = jnp.sum(capacity * eye, axis=1, keepdims=True)
    root_row, root_col = lax.rsqrt(diag_row), lax.rsqrt(diag_col)
    scaled = 0.5 * (capacity + capacity.T) * root_row * root_col
    sums = jnp.sum(jnp.abs(scaled), axis=0, keepdims=True)
    high = jnp.broadcast_to(jnp.max(sums, axis=1, keepdims=True), (1, rank))
    low = 0.99 * jnp.min(extra / diag_row, axis=1, keepdims=True)
    low = jnp.broadcast_to(low, (1, rank))
    rhs = root_col * front[:, :width]
    return root_col * mm(fixed_inverse(scaled, low, high, doublings), rhs), None


def tree_kernel(rank, levels, inner_bits, doublings, extra_ref, solved_ref, *refs):
    pairs = [(k, j) for k in range(levels) for j in range(k, levels)]
    number = {pair: index for index, pair in enumerate(pairs)}
    first, refs = refs[:levels], refs[levels:]
    if doublings:
        (rest_ref, coef_ref, state_ref), refs = refs[:3], refs[3:]
    else:
        (rest_ref, coef_ref, flag_ref, state_ref), refs = refs[:4], refs[4:]
    landed = dict(zip(pairs, refs[: len(pairs)]))
    later = pairs[levels:]
    own = dict(zip(pairs[:levels], first))
    own.update(zip(later, refs[len(pairs) : len(pairs) + len(later)]))
    send_sem, recv_sem, load_sem = refs[-3:]
    load = pltpu.make_async_copy(solved_ref, state_ref, load_sem)
    load.start()
    widths = [solved_ref.shape[1] - rank * j for j in range(levels)]
    heights = [packed_rows(rank, wide) for wide in widths]
    if not doublings:
        for k in range(1, levels):
            own[k, k][heights[k] :, :] = jnp.zeros((FLAG_ROWS, LANES), jnp.float32)

    group, inner = lax.axis_index("group"), lax.axis_index("inner")

    def partner(level):
        if level < inner_bits:
            mask = 2**level
            return (group, inner + mask * (1 - 2 * ((inner // mask) % 2)))
        mask = 2 ** (level - inner_bits)
        return (group + mask * (1 - 2 * ((group // mask) % 2)), inner)

    partners = [partner(level) for level in range(levels)]

    def copy_of(k, j):
        return pltpu.make_async_remote_copy(
            src_ref=own[k, j],
            dst_ref=landed[k, j],
            send_sem=send_sem.at[number[k, j]],
            recv_sem=recv_sem.at[number[k, j]],
            device_id=partners[k],
            device_id_type=pl.DeviceIdType.MESH,
        )

    barrier = pltpu.get_barrier_semaphore()
    for other in partners:
        pl.semaphore_signal(
            barrier, inc=1, device_id=other, device_id_type=pl.DeviceIdType.MESH
        )
    pl.semaphore_wait(barrier, levels)

    for j in range(min(levels, 2)):
        copy_of(0, j).start()
    bad = jnp.zeros((1, rank), jnp.float32)
    for k in range(levels):
        copy_of(k, k).wait_recv()
        if k == 0:
            for j in range(2, levels):
                copy_of(0, j).start()
        height = heights[k]
        front = own[k, k][:height, :] + landed[k, k][:height, :]
        front = unpack(front, rank, widths[k])
        wide = front.shape[1] - rank
        base = wide - rank * (levels - 1 - k)
        turned = front[:, base:wide].T if k + 1 < levels else None
        coef, worst = capacity_solve(
            front,
            extra_ref[k : k + 1, :],
            rank,
            doublings,
            5 if k == 0 else 4,
        )
        if not doublings:
            if k > 0:
                flags = jnp.maximum(own[k, k][height:, :], landed[k, k][height:, :])
                bad = jnp.maximum(bad, flags[:1, :rank])
            bad = jnp.maximum(bad, worst)
        if k + 1 == levels:
            coef_ref[...] = coef
        for j in range(k + 1, levels):
            rows = rank * (levels - 1 - j)
            update = pack(mm(turned[rows : rows + rank, :], coef[:, : widths[j]]))
            copy_of(k, j).wait_recv()
            total = own[k, j][...] + landed[k, j][...] - update
            own[k + 1, j][: heights[j], :] = total
            if j == k + 1 and not doublings:
                own[k + 1, j][heights[j] :, :rank] = jnp.broadcast_to(
                    bad, (FLAG_ROWS, rank)
                )
            copy_of(k + 1, j).start()
            if j == k + 1:
                if k == 0:
                    load.wait()
                target = rest_ref if k + 2 == levels else state_ref
                target[:, :wide] = state_ref[:, :wide] - mm(
                    state_ref[:, wide : wide + rank], coef
                )
    if not doublings:
        flag_ref[0] = jnp.max(bad)
    for pair in pairs:
        copy_of(*pair).wait_send()


def call_tree(extra, solved, blocks, inner_bits, doublings):
    levels, rank = extra.shape
    rows, width = solved.shape
    right = width - rank * levels
    f32 = jnp.float32
    pairs = [(k, j) for k in range(levels) for j in range(k, levels)]
    flag_rows = 0 if doublings else FLAG_ROWS
    landed = [
        pltpu.VMEM(
            (
                packed_rows(rank, width - rank * j) + (flag_rows if j == k > 0 else 0),
                LANES,
            ),
            f32,
        )
        for k, j in pairs
    ]
    result = [
        jax.ShapeDtypeStruct((rows, right + rank), f32),
        jax.ShapeDtypeStruct((rank, right), f32),
    ]
    if not doublings:
        result.append(jax.ShapeDtypeStruct((1,), f32))
    return pl.pallas_call(
        functools.partial(tree_kernel, rank, levels, inner_bits, doublings),
        out_shape=result,
        in_specs=[VMEM, pl.BlockSpec(memory_space=pl.ANY)] + [VMEM] * levels,
        out_specs=[VMEM] * 2 + [pl.BlockSpec(memory_space=pltpu.SMEM)] * (len(result) - 2),
        scratch_shapes=[pltpu.VMEM((rows, width), f32)]
        + landed
        + landed[levels:]
        + [pltpu.SemaphoreType.DMA((len(pairs),))] * 2
        + [pltpu.SemaphoreType.DMA],
        compiler_params=pltpu.CompilerParams(
            collective_id=1 if doublings else 0,
            has_side_effects=True,
            vmem_limit_bytes=60 * 2**20,
        ),
        name="careful" if doublings else "tree",
    )(extra, solved, *blocks)


def last_kernel(rest_ref, coef_ref, out_ref):
    width = out_ref.shape[1]
    out_ref[...] = rest_ref[:, :width] - mm(rest_ref[:, width:], coef_ref[...])


def last_update(rest, coef):
    return pl.pallas_call(
        last_kernel,
        out_shape=jax.ShapeDtypeStruct((rest.shape[0], coef.shape[1]), jnp.float32),
        in_specs=[VMEM] * 2,
        out_specs=VMEM,
        compiler_params=pltpu.CompilerParams(vmem_limit_bytes=60 * 2**20),
        name="last",
    )(rest, coef)


def per_device(leaf_blocks, bases, targets, coupling):
    levels, rank = coupling.shape
    rows, size = leaf_blocks.shape
    right = targets.shape[1]
    width = right + rank * levels
    inner_bits = lax.axis_size("inner").bit_length() - 1
    f32 = jnp.float32
    widths = [width - rank * level for level in range(levels)]
    solved, extra, *blocks = pl.pallas_call(
        functools.partial(leaf_kernel, rank, levels),
        out_shape=[
            jax.ShapeDtypeStruct((rows, width), f32),
            jax.ShapeDtypeStruct((levels, rank), f32),
        ]
        + [jax.ShapeDtypeStruct((packed_rows(rank, wide), LANES), f32) for wide in widths],
        in_specs=[VMEM] * 4,
        out_specs=[VMEM] * (2 + levels),
        scratch_shapes=[pltpu.VMEM((2 * size, size), f32)],
        compiler_params=pltpu.CompilerParams(vmem_limit_bytes=60 * 2**20),
        name="leaf",
    )(leaf_blocks, bases.T, targets, coupling)
    worst = rank * (4.0 * rows * 2**levels / EIGEN_MIN + 1.0)
    doublings = math.ceil(math.log2(math.sqrt(worst) * 4.1))
    rest, coef, flag = call_tree(extra, solved, blocks, inner_bits, 0)

    def careful():
        return tuple(call_tree(extra, solved, blocks, inner_bits, doublings))

    rest, coef = lax.cond(flag[0] <= RESIDUAL_MAX, lambda: (rest, coef), careful)
    return last_update(rest, coef)


def solution(mesh):
    rows = P(("group", "inner"), None)
    return jax.shard_map(
        per_device,
        mesh=mesh,
        in_specs=(rows, rows, rows, P()),
        out_specs=rows,
        check_vma=False,
    )
```

```python
import functools
import math

import jax
import jax.numpy as jnp
from jax import lax
from jax.experimental import pallas as pl
from jax.experimental.pallas import tpu as pltpu
from jax.sharding import PartitionSpec as P

EIGEN_MIN = 0.4
LEAF_TOL = 3e-4
RESIDUAL_MAX = 1e-3
FLAG_ROWS = 8
RELAX = 1.5
LANES = 128
VMEM = pl.BlockSpec(memory_space=pltpu.VMEM)


def mm(first, second):
    return jnp.dot(
        first,
        second,
        precision=lax.Precision.HIGHEST,
        preferred_element_type=jnp.float32,
    )


def split(value):
    high = value.astype(jnp.bfloat16)
    return high, (value - high.astype(jnp.float32)).astype(jnp.bfloat16)


def mm3(first, second):
    (a_high, a_low), (b_high, b_low) = split(first), split(second)
    dot = functools.partial(jnp.dot, preferred_element_type=jnp.float32)
    return dot(a_high, b_high) + (dot(a_high, b_low) + dot(a_low, b_high))


def mm_t(first, second):
    return lax.dot_general(
        first,
        second,
        (((0,), (0,)), ((), ())),
        precision=lax.Precision.HIGHEST,
        preferred_element_type=jnp.float32,
    )


def packed_rows(rank, width):
    return rank * (width // LANES) + (rank // 2 if width % LANES else 0)


def pack(value):
    rank, width = value.shape
    full = width // LANES
    tiles = [value[:, LANES * t : LANES * (t + 1)] for t in range(full)]
    if width % LANES:
        tail = value[:, LANES * full :]
        tiles.append(jnp.concatenate([tail[: rank // 2], tail[rank // 2 :]], axis=1))
    return jnp.concatenate(tiles, axis=0)


def unpack(value, rank, width):
    full = width // LANES
    tiles = [value[rank * t : rank * (t + 1), :] for t in range(full)]
    if width % LANES:
        tail = value[rank * full :, :]
        half = LANES // 2
        tiles.append(jnp.concatenate([tail[:, :half], tail[:, half:]], axis=0))
    return jnp.concatenate(tiles, axis=1)


def identity(size):
    rows = lax.broadcasted_iota(jnp.int32, (size, size), 0)
    cols = lax.broadcasted_iota(jnp.int32, (size, size), 1)
    return jnp.where(rows == cols, 1.0, 0.0).astype(jnp.float32)


def spd_solve(matrix, rhs, low, high, pair_ref):
    size = matrix.shape[0]
    eye = identity(size)
    alpha = 2.0 / (low + high)
    rho = (high - low) / (high + low)
    scale = 2.0 / (2.0 - rho * rho)
    residual = eye - alpha * matrix
    pair_ref[:size, :] = (1.0 - scale) * eye + scale * mm3(residual, residual)
    pair_ref[size:, :] = (scale * alpha) * (eye + residual)

    def cond(rho):
        return rho > LEAF_TOL

    def body(rho):
        square = rho * rho
        scale = 2.0 / (2.0 - square)
        pair = pair_ref[...]
        product = mm3(pair, pair[:size])
        pair_ref[:size, :] = (1.0 - scale) * eye + scale * product[:size]
        pair_ref[size:, :] = scale * (pair[size:] + product[size:])
        return square / (2.0 - square)

    lax.while_loop(cond, body, rho * rho / (2.0 - rho * rho))

    @pl.when(high > 100.0 * low)
    def _():
        for _ in range(2):
            inverse = pair_ref[size:, :]
            pair_ref[size:, :] = inverse + mm(inverse, eye - mm(matrix, inverse))

    both = mm(pair_ref[size:, :], jnp.concatenate([matrix, rhs], axis=1))
    found = both[:, size:]
    return found + mm3(eye - both[:, :size], found)


def leaf_kernel(rank, levels, leaf_ref, bases_ref, targets_ref, coupling_ref, *rest):
    solved_ref, extra_ref, rest = rest[0], rest[1], rest[2:]
    blocks, pair_ref = rest[:levels], rest[levels]
    extra_ref[...] = 1.0 / coupling_ref[...]
    matrix = leaf_ref[...]
    high = jnp.max(jnp.sum(jnp.abs(matrix), axis=0, keepdims=True))
    flipped = jnp.concatenate(
        [
            bases_ref[rank * level : rank * (level + 1), :]
            for level in reversed(range(levels))
        ],
        axis=0,
    )
    rhs = jnp.concatenate([targets_ref[...], flipped.T], axis=1)
    high = jnp.maximum(high, 2 * EIGEN_MIN)
    solved = spd_solve(matrix, rhs, EIGEN_MIN, high, pair_ref)
    solved_ref[...] = solved
    gram = mm(bases_ref[...], solved)
    for level in range(levels):
        width = solved.shape[1] - rank * level
        blocks[level][...] = pack(gram[rank * level : rank * (level + 1), :width])


def fixed_inverse(matrix, low, high, doublings):
    size = matrix.shape[0]
    eye = identity(size)
    alpha = 2.0 / (low + high)
    rho = (high - low) / (high + low)
    residual = eye - alpha * matrix
    inverse = alpha * eye
    for _ in range(doublings):
        square = rho * rho
        scale = 2.0 / (2.0 - square)
        rho = square / (2.0 - square)
        product = mm(jnp.concatenate([residual, inverse], axis=0), residual)
        inverse = scale * (inverse + product[size:])
        residual = (1.0 - scale) * eye + scale * product[:size]
    return inverse + mm(inverse, eye - mm(matrix, inverse))


def quick_solve(matrix, rhs, squarings):
    size = matrix.shape[0]
    eye = identity(size)
    residual = eye - matrix * (
        RELAX / jnp.sum(jnp.abs(matrix), axis=0, keepdims=True)
    )
    inverse = eye * (RELAX / jnp.sum(jnp.abs(matrix), axis=0, keepdims=True))
    for _ in range(squarings - 1):
        product = mm3(jnp.concatenate([residual, inverse], axis=0), residual)
        inverse = inverse + product[size:]
        residual = product[:size]
    inverse = inverse + mm3(inverse, residual)
    both = mm(inverse, jnp.concatenate([rhs, matrix], axis=1))
    found = both[:, : rhs.shape[1]]
    error = eye - both[:, rhs.shape[1] :]
    worst = jnp.sum(jnp.abs(error), axis=0, keepdims=True)
    return found + mm3(error, found), worst


def capacity_solve(front, extra, rank, doublings, squarings):
    width = front.shape[1] - rank
    eye = identity(rank)
    capacity = front[:, width:] + eye * extra
    if not doublings:
        return quick_solve(capacity, front[:, :width], squarings)
    diag_row = jnp.sum(capacity * eye, axis=0, keepdims=True)
    diag_col = jnp.sum(capacity * eye, axis=1, keepdims=True)
    root_row, root_col = lax.rsqrt(diag_row), lax.rsqrt(diag_col)
    scaled = 0.5 * (capacity + capacity.T) * root_row * root_col
    sums = jnp.sum(jnp.abs(scaled), axis=0, keepdims=True)
    high = jnp.broadcast_to(jnp.max(sums, axis=1, keepdims=True), (1, rank))
    low = 0.99 * jnp.min(extra / diag_row, axis=1, keepdims=True)
    low = jnp.broadcast_to(low, (1, rank))
    rhs = root_col * front[:, :width]
    return root_col * mm(fixed_inverse(scaled, low, high, doublings), rhs), None


def tree_kernel(rank, levels, inner_bits, doublings, extra_ref, solved_ref, *refs):
    pairs = [(k, j) for k in range(levels) for j in range(k, levels)]
    number = {pair: index for index, pair in enumerate(pairs)}
    first, refs = refs[:levels], refs[levels:]
    if doublings:
        (rest_ref, coef_ref, state_ref), refs = refs[:3], refs[3:]
    else:
        (rest_ref, coef_ref, flag_ref, state_ref), refs = refs[:4], refs[4:]
    landed = dict(zip(pairs, refs[: len(pairs)]))
    later = pairs[levels:]
    own = dict(zip(pairs[:levels], first))
    own.update(zip(later, refs[len(pairs) : len(pairs) + len(later)]))
    send_sem, recv_sem, load_sem = refs[-3:]
    load = pltpu.make_async_copy(solved_ref, state_ref, load_sem)
    load.start()
    widths = [solved_ref.shape[1] - rank * j for j in range(levels)]
    heights = [packed_rows(rank, wide) for wide in widths]
    if not doublings:
        for k in range(1, levels):
            own[k, k][heights[k] :, :] = jnp.zeros((FLAG_ROWS, LANES), jnp.float32)

    group, inner = lax.axis_index("group"), lax.axis_index("inner")

    def partner(level):
        if level < inner_bits:
            mask = 2**level
            return (group, inner + mask * (1 - 2 * ((inner // mask) % 2)))
        mask = 2 ** (level - inner_bits)
        return (group + mask * (1 - 2 * ((group // mask) % 2)), inner)

    partners = [partner(level) for level in range(levels)]

    def copy_of(k, j):
        return pltpu.make_async_remote_copy(
            src_ref=own[k, j],
            dst_ref=landed[k, j],
            send_sem=send_sem.at[number[k, j]],
            recv_sem=recv_sem.at[number[k, j]],
            device_id=partners[k],
            device_id_type=pl.DeviceIdType.MESH,
        )

    barrier = pltpu.get_barrier_semaphore()
    for other in partners:
        pl.semaphore_signal(
            barrier, inc=1, device_id=other, device_id_type=pl.DeviceIdType.MESH
        )
    pl.semaphore_wait(barrier, levels)

    for j in range(min(levels, 2)):
        copy_of(0, j).start()
    bad = jnp.zeros((1, rank), jnp.float32)
    for k in range(levels):
        copy_of(k, k).wait_recv()
        if k == 0:
            for j in range(2, levels):
                copy_of(0, j).start()
        height = heights[k]
        front = own[k, k][:height, :] + landed[k, k][:height, :]
        front = unpack(front, rank, widths[k])
        wide = front.shape[1] - rank
        base = wide - rank * (levels - 1 - k)
        turned = front[:, base:wide].T if k + 1 < levels else None
        coef, worst = capacity_solve(
            front,
            extra_ref[k : k + 1, :],
            rank,
            doublings,
            5 if k == 0 else 4,
        )
        if not doublings:
            if k > 0:
                flags = jnp.maximum(own[k, k][height:, :], landed[k, k][height:, :])
                bad = jnp.maximum(bad, flags[:1, :rank])
            bad = jnp.maximum(bad, worst)
        if k + 1 == levels:
            coef_ref[...] = coef
        for j in range(k + 1, levels):
            rows = rank * (levels - 1 - j)
            update = pack(mm(turned[rows : rows + rank, :], coef[:, : widths[j]]))
            copy_of(k, j).wait_recv()
            total = own[k, j][...] + landed[k, j][...] - update
            own[k + 1, j][: heights[j], :] = total
            if j == k + 1 and not doublings:
                own[k + 1, j][heights[j] :, :rank] = jnp.broadcast_to(
                    bad, (FLAG_ROWS, rank)
                )
            copy_of(k + 1, j).start()
        if k + 1 < levels:
            if k == 0:
                load.wait()
            target = rest_ref if k + 2 == levels else state_ref
            target[:, :wide] = state_ref[:, :wide] - mm(
                state_ref[:, wide : wide + rank], coef
            )
    if not doublings:
        flag_ref[0] = jnp.max(bad)
    for pair in pairs:
        copy_of(*pair).wait_send()


def call_tree(extra, solved, blocks, inner_bits, doublings):
    levels, rank = extra.shape
    rows, width = solved.shape
    right = width - rank * levels
    f32 = jnp.float32
    pairs = [(k, j) for k in range(levels) for j in range(k, levels)]
    flag_rows = 0 if doublings else FLAG_ROWS
    landed = [
        pltpu.VMEM(
            (
                packed_rows(rank, width - rank * j) + (flag_rows if j == k > 0 else 0),
                LANES,
            ),
            f32,
        )
        for k, j in pairs
    ]
    result = [
        jax.ShapeDtypeStruct((rows, right + rank), f32),
        jax.ShapeDtypeStruct((rank, right), f32),
    ]
    if not doublings:
        result.append(jax.ShapeDtypeStruct((1,), f32))
    return pl.pallas_call(
        functools.partial(tree_kernel, rank, levels, inner_bits, doublings),
        out_shape=result,
        in_specs=[VMEM, pl.BlockSpec(memory_space=pl.ANY)] + [VMEM] * levels,
        out_specs=[VMEM] * 2 + [pl.BlockSpec(memory_space=pltpu.SMEM)] * (len(result) - 2),
        scratch_shapes=[pltpu.VMEM((rows, width), f32)]
        + landed
        + landed[levels:]
        + [pltpu.SemaphoreType.DMA((len(pairs),))] * 2
        + [pltpu.SemaphoreType.DMA],
        compiler_params=pltpu.CompilerParams(
            collective_id=1 if doublings else 0,
            has_side_effects=True,
            vmem_limit_bytes=60 * 2**20,
        ),
        name="careful" if doublings else "tree",
    )(extra, solved, *blocks)


def last_kernel(rest_ref, coef_ref, out_ref):
    width = out_ref.shape[1]
    out_ref[...] = rest_ref[:, :width] - mm(rest_ref[:, width:], coef_ref[...])


def last_update(rest, coef):
    return pl.pallas_call(
        last_kernel,
        out_shape=jax.ShapeDtypeStruct((rest.shape[0], coef.shape[1]), jnp.float32),
        in_specs=[VMEM] * 2,
        out_specs=VMEM,
        compiler_params=pltpu.CompilerParams(vmem_limit_bytes=60 * 2**20),
        name="last",
    )(rest, coef)


def per_device(leaf_blocks, bases, targets, coupling):
    levels, rank = coupling.shape
    rows, size = leaf_blocks.shape
    right = targets.shape[1]
    width = right + rank * levels
    inner_bits = lax.axis_size("inner").bit_length() - 1
    f32 = jnp.float32
    widths = [width - rank * level for level in range(levels)]
    solved, extra, *blocks = pl.pallas_call(
        functools.partial(leaf_kernel, rank, levels),
        out_shape=[
            jax.ShapeDtypeStruct((rows, width), f32),
            jax.ShapeDtypeStruct((levels, rank), f32),
        ]
        + [jax.ShapeDtypeStruct((packed_rows(rank, wide), LANES), f32) for wide in widths],
        in_specs=[VMEM] * 4,
        out_specs=[VMEM] * (2 + levels),
        scratch_shapes=[pltpu.VMEM((2 * size, size), f32)],
        compiler_params=pltpu.CompilerParams(vmem_limit_bytes=60 * 2**20),
        name="leaf",
    )(leaf_blocks, bases.T, targets, coupling)
    worst = rank * (4.0 * rows * 2**levels / EIGEN_MIN + 1.0)
    doublings = math.ceil(math.log2(math.sqrt(worst) * 4.1))
    rest, coef, flag = call_tree(extra, solved, blocks, inner_bits, 0)

    def careful():
        return tuple(call_tree(extra, solved, blocks, inner_bits, doublings))

    rest, coef = lax.cond(flag[0] <= RESIDUAL_MAX, lambda: (rest, coef), careful)
    return last_update(rest, coef)


def solution(mesh):
    rows = P(("group", "inner"), None)
    return jax.shard_map(
        per_device,
        mesh=mesh,
        in_specs=(rows, rows, rows, P()),
        out_specs=rows,
        check_vma=False,
    )
```
